32 devices in a mesh: groups: 2 (over y), seq: 4 (over z), head: 4 (over x, core).
Axes of the slice: x: 2, y: 2, z: 4, core: 2. Of those that a mesh axis runs over, the one named last changes fastest.
Arguments:
- queries: bfloat16 [1024, 2048], P(('groups', 'seq', 'head')), parts along dimension 0, may hold values from -6 to 6
- keys: bfloat16 [1024, 2048], P(('groups', 'seq', 'head')), parts along dimension 0, may hold values from -6 to 6
- values: bfloat16 [1024, 4096], P(('groups', 'seq', 'head')), parts along dimension 0, may hold values from -6 to 6
- cotangent: bfloat16 [1024, 4096], P(('groups', 'seq', 'head')), parts along dimension 0, may hold values from -6 to 6
- igate: float32 [8, 1024], P('head', ('groups', 'seq')), parts along dimension 1, may hold values from -3 to 1
- fgate: float32 [8, 1024], P('head', ('groups', 'seq')), parts along dimension 1, may hold values from 0 to 10
- lengths: int32 [8], P(('groups', 'seq')), parts along dimension 0, may hold values from 1 to 128, 256 in all
Outputs:
- hidden_out: bfloat16 [1024, 4096], P(('groups', 'seq', 'head')), parts along dimension 0
- grad_queries: bfloat16 [1024, 2048], P(('groups', 'seq', 'head')), parts along dimension 0
- grad_keys: bfloat16 [1024, 2048], P(('groups', 'seq', 'head')), parts along dimension 0
- grad_values: bfloat16 [1024, 4096], P(('groups', 'seq', 'head')), parts along dimension 0
- grad_igate: float32 [8, 1024], P('head', ('groups', 'seq')), parts along dimension 1
- grad_fgate: float32 [8, 1024], P('head', ('groups', 'seq')), parts along dimension 1
The draws below stay inside these ranges and needn't reach their ends.
There are 2 independent parts, one for each index of `groups`. The reference program is written for one: setup_inputs(seed, part) draws one part's arguments, and reference() takes and returns one part's arrays. A program takes and returns all parts, laid end to end along the dimension named above; each array names one. Nothing has to cross between parts.
All inputs are finite; a program needn't handle non-finite values. No bound on the sum of `lengths` on one device may be relied on, other than what follows from the above.
Results may differ from the reference program's by a relative error of at most 0.001.
Values may be sent and summed in bfloat16 or wider, within the bound.
No kernel may reach another device: no remote copies, remote signals or barrier semaphores. Data moves between devices by JAX's collectives and lax.ppermute only.
A program may use at most 128 MiB of HBM per device.

```python
import math
import jax
import jax.numpy as jnp
import numpy as np
from jax import lax

MLSTM_HEADS = 8
QK_DIM = 256
V_DIM = 512
BLOCK_ROWS = 64
ROLLOUT_ROW_SLOTS = 128
ROWS = 512
N_SEQ = 4


def draw_fgate(key, part):
    key = jax.random.fold_in(key, 11)
    random_key_start, random_key_shift, random_key_jagged, random_key_spike, random_key_height = jax.random.split(key, 5)
    episode_rollouts = ROWS // ROLLOUT_ROW_SLOTS
    head_start_index = jax.random.uniform(random_key_start, (MLSTM_HEADS, 1, 1), jnp.float32, 3.5, 8.0)
    shift_amount = jax.random.uniform(random_key_shift, (MLSTM_HEADS, episode_rollouts, 1), jnp.float32, -0.7, 0.7)
    jaggedness = jax.random.uniform(random_key_jagged, (MLSTM_HEADS, episode_rollouts, ROLLOUT_ROW_SLOTS), jnp.float32, -0.5, 0.5)
    spike_mask = jax.random.bernoulli(random_key_spike, 0.01, (MLSTM_HEADS, episode_rollouts, ROLLOUT_ROW_SLOTS))
    spike_level = jax.random.uniform(random_key_height, (MLSTM_HEADS, episode_rollouts, ROLLOUT_ROW_SLOTS), jnp.float32, 0.0, 1.4)
    layer_output = jnp.where(spike_mask, spike_level, head_start_index + shift_amount + jaggedness)
    return layer_output.reshape(MLSTM_HEADS, ROWS).astype(jnp.float32)


def shard_levels(key, dims, cuts, smallest, top_value):
    def one(position, shards_of):
        steps = jax.random.uniform(jax.random.fold_in(jax.random.fold_in(key, 6), position), (shards_of,), jnp.float32, smallest / len(cuts), top_value / len(cuts))
        return jnp.repeat(jnp.exp(steps), dims[position] // shards_of).reshape((-1,) + (1,) * (len(dims) - position - 1))

    loudness = one(*cuts[0])
    for cut in cuts[1:]:
        loudness = loudness * one(*cut)
    return loudness


def profile(amount, total, most, skew):
    loads = [(1 << 20) // math.isqrt(grade ** skew) + 1 for grade in range(2, amount + 1)]
    surplus, given = total - most - (amount - 1), [1] * (amount - 1)
    while surplus > 0:
        candidates = [i for i in range(amount - 1) if given[i] < most]
        pool, budget = sum([loads[i] for i in candidates]), surplus
        for i in candidates:
            addition = min(most - given[i], max(1, budget * loads[i] // pool), surplus)
            given[i] = given[i] + addition
            surplus = surplus - addition
    return np.array([most] + given)


def uneven(own_key, number_of, total, reach, skew):
    if number_of == 2:
        one = jax.random.randint(own_key, (), max(1, total - reach), min(reach, total - 1) + 1)
        return jnp.stack([one, total - one])
    tallies = jnp.asarray(profile(number_of, total, reach, skew), jnp.int32)
    pairs = (number_of - 1) // 2
    donor, sink = tallies[1:1 + 2 * pairs:2], tallies[2:2 + 2 * pairs:2]
    slack = jnp.minimum(donor - 1, reach - sink)
    passed = jax.random.randint(jax.random.fold_in(own_key, 1), (pairs,), 0, 1 << 20) % (slack + 1)
    tallies = tallies.at[1:1 + 2 * pairs:2].set(donor - passed).at[2:2 + 2 * pairs:2].set(sink + passed)
    return tallies[jax.random.permutation(jax.random.fold_in(own_key, 2), number_of)]


def gaussian(key, shape, deviation, bound, cuts=(), kind=jnp.bfloat16):
    gain = shard_levels(key, shape, cuts, -0.22, 0.18) if cuts else 1.0
    result = jax.random.normal(key, shape, jnp.float32) * deviation * gain
    return jnp.minimum(jnp.maximum(result, -bound), bound).astype(kind)


def setup_inputs(seed: int = 0, part: int = 0) -> dict:
    arg_keys = jax.random.split(jax.random.key(seed), 8)
    part_keys = jax.random.split(jax.random.fold_in(arg_keys[7], part), 8)
    queries = gaussian(part_keys[0], (ROWS, MLSTM_HEADS * QK_DIM), 1.0, 6.0, ((0, 16),))
    keys = gaussian(part_keys[1], (ROWS, MLSTM_HEADS * QK_DIM), 1.0, 6.0, ((0, 16),))
    values = gaussian(part_keys[2], (ROWS, MLSTM_HEADS * V_DIM), 1.0, 6.0, ((0, 16),))
    cotangent = gaussian(part_keys[3], (ROWS, MLSTM_HEADS * V_DIM), 1.0, 6.0, ((0, 16),))
    igate = jnp.clip(-3.0 + 4.0 * jax.random.uniform(part_keys[4], (MLSTM_HEADS, ROWS), jnp.float32) ** shard_levels(part_keys[4], (MLSTM_HEADS, ROWS), ((0, 4), (1, 4)), -0.2, 0.2), -3.0, 1.0)
    fgate = draw_fgate(jax.random.fold_in(jax.random.fold_in(arg_keys[7], part), 71), part)
    lengths = uneven(part_keys[6], N_SEQ, N_SEQ * ROLLOUT_ROW_SLOTS // 4 + ROLLOUT_ROW_SLOTS, ROLLOUT_ROW_SLOTS, 1).astype(jnp.int32)
    return {"queries": queries, "keys": keys, "values": values, "cotangent": cotangent, "igate": igate, "fgate": fgate, "lengths": lengths}


HIGHEST_PRECISION = lax.Precision.HIGHEST

def product(left, right):
    return jnp.dot(left, right, precision=HIGHEST_PRECISION, preferred_element_type=jnp.float32)

def block_step(carried, block_data):

    def active(operand):
        (memory, norm_state), (q_rows, k_rows, v_rows, in_gate, forget_gate, live_mask) = operand
        block_rows = q_rows.shape[0]
        scaled_keys = k_rows * k_rows.shape[1] ** (-0.5)
        cumulative = jnp.cumsum(jax.nn.log_sigmoid(forget_gate) * live_mask)
        inflow = jnp.exp(in_gate) * live_mask
        causal_mask = jnp.arange(block_rows)[:, None] >= jnp.arange(block_rows)[None, :]
        spread_log = cumulative[:, None] - cumulative[None, :]
        decay_table = jnp.where(causal_mask, jnp.exp(jnp.where(causal_mask, spread_log, 0.0)), 0.0)
        scores = product(q_rows, scaled_keys.T) * decay_table * inflow[None, :]
        front_decay = jnp.exp(cumulative)
        numerator = front_decay[:, None] * product(q_rows, memory) + product(scores, v_rows)
        denominator = front_decay * product(q_rows, norm_state) + lax.optimization_barrier(jnp.sum(scores, axis=1))
        hidden = numerator / jnp.maximum(jnp.abs(denominator), 1.0)[:, None] * live_mask[:, None]
        tail_weight = jnp.exp(cumulative[-1] - cumulative) * inflow
        memory = front_decay[-1] * memory + product((scaled_keys * tail_weight[:, None]).T, v_rows)
        norm_state = front_decay[-1] * norm_state + product(tail_weight, scaled_keys)
        return ((memory, norm_state), hidden)

    def skipped(operand):
        state_pair, pieces = operand
        return (state_pair, jnp.zeros((pieces[0].shape[0], pieces[2].shape[1]), jnp.float32))
    return lax.cond(block_data[5][0] > 0, active, skipped, (carried, block_data))

def run_scan(q_rows, k_rows, v_rows, in_gate, forget_gate, live_mask, memory, norm_state):
    block_count = q_rows.shape[0] // BLOCK_ROWS

    def to_blocks(tensor):
        return tensor.reshape((block_count, BLOCK_ROWS) + tensor.shape[1:])
    pieces = tuple((to_blocks(tensor) for tensor in (q_rows, k_rows, v_rows, in_gate, forget_gate, live_mask)))
    final_state, hidden = lax.scan(block_step, (memory, norm_state), pieces)
    return (hidden.reshape(q_rows.shape[0], v_rows.shape[1]), final_state)

def one_head(inputs):
    q_rows, k_rows, v_rows, grad_rows, in_gate, forget_gate, live_mask = inputs
    zero_memory = jnp.zeros((QK_DIM, V_DIM), jnp.float32)
    zero_norm = jnp.zeros((QK_DIM,), jnp.float32)

    def forward(q_part, k_part, v_part, i_part, f_part):
        return run_scan(q_part, k_part, v_part, i_part, f_part, live_mask, zero_memory, zero_norm)[0]
    hidden, pull = jax.vjp(forward, q_rows, k_rows, v_rows, in_gate, forget_gate)
    return (hidden,) + tuple(pull(grad_rows))

def reference(queries, keys, values, cotangent, igate, fgate, lengths):

    def head_layout(tensor, width):
        return tensor.astype(jnp.float32).reshape(N_SEQ, ROLLOUT_ROW_SLOTS, MLSTM_HEADS, width).transpose(0, 2, 1, 3).reshape(N_SEQ * MLSTM_HEADS, ROLLOUT_ROW_SLOTS, width)

    def gate_layout(tensor):
        return tensor.reshape(MLSTM_HEADS, N_SEQ, ROLLOUT_ROW_SLOTS).transpose(1, 0, 2).reshape(N_SEQ * MLSTM_HEADS, ROLLOUT_ROW_SLOTS)

    def row_layout(tensor, width):
        return tensor.reshape(N_SEQ, MLSTM_HEADS, ROLLOUT_ROW_SLOTS, width).transpose(0, 2, 1, 3).reshape(N_SEQ * ROLLOUT_ROW_SLOTS, MLSTM_HEADS * width).astype(jnp.bfloat16)

    def gate_back(tensor):
        return tensor.reshape(N_SEQ, MLSTM_HEADS, ROLLOUT_ROW_SLOTS).transpose(1, 0, 2).reshape(MLSTM_HEADS, N_SEQ * ROLLOUT_ROW_SLOTS)
    positions = jnp.arange(ROLLOUT_ROW_SLOTS, dtype=jnp.int32)
    live_rows = (positions[None, :] < lengths[:, None]).astype(jnp.float32)
    live_rows = jnp.repeat(live_rows, MLSTM_HEADS, axis=0)
    results = lax.map(one_head, (head_layout(queries, QK_DIM), head_layout(keys, QK_DIM), head_layout(values, V_DIM), head_layout(cotangent, V_DIM), gate_layout(igate), gate_layout(fgate), live_rows))
    hidden, grad_q, grad_k, grad_v, grad_in, grad_forget = results
    return (row_layout(hidden, V_DIM), row_layout(grad_q, QK_DIM), row_layout(grad_k, QK_DIM), row_layout(grad_v, V_DIM), gate_back(grad_in), gate_back(grad_forget))
```

```python
import functools

import jax
import jax.numpy as jnp
from jax import lax
from jax.experimental import pallas as pl
from jax.experimental.pallas import tpu as pltpu
from jax.sharding import PartitionSpec as P

FAR = -1e30


def dot(left, right, contract):
    return lax.dot_general(left, right, (contract, ((), ())), preferred_element_type=jnp.float32)


def halves(value):
    high = value.astype(jnp.bfloat16)
    return high, (value - high.astype(jnp.float32)).astype(jnp.bfloat16)


def wide_dot(left, right, contract):
    high, low = halves(left)
    return dot(high, right, contract) + dot(low, right, contract)


NN = ((1,), (0,))
NT = ((1,), (1,))
TN = ((0,), (0,))


def log_sigmoid(value):
    return jnp.minimum(value, 0.0) - jnp.log(1.0 + jnp.exp(-jnp.abs(value)))


def decay(in_gate, forget_gate, length, scale):
    size = in_gate.shape[1]
    rows = lax.broadcasted_iota(jnp.int32, (size, size), 0)
    cols = lax.broadcasted_iota(jnp.int32, (size, size), 1)
    logs = jnp.where(cols[:1] < length, log_sigmoid(forget_gate), 0.0)
    total_col = jnp.sum(jnp.where(cols <= rows, logs, 0.0), axis=1, keepdims=True)
    total_row = jnp.sum(jnp.where(cols == rows, total_col, 0.0), axis=0, keepdims=True)
    mask = (cols <= rows) & (rows < length)
    return jnp.exp(jnp.where(mask, total_col - total_row, FAR)) * (jnp.exp(in_gate) * scale)


def whole_kernel(heads, qk, vw, length_ref, x_ref, ig_ref, fg_ref, out_ref, gi_ref, gf_ref):
    length = length_ref[0]
    size = x_ref.shape[0]
    rows = lax.broadcasted_iota(jnp.int32, (size, size), 0)
    cols = lax.broadcasted_iota(jnp.int32, (size, size), 1)
    for head in range(heads):
        q = x_ref[:, head * qk : (head + 1) * qk]
        k = x_ref[:, (heads + head) * qk : (heads + head + 1) * qk]
        v0 = 2 * heads * qk + head * vw
        g0 = v0 + heads * vw
        v = x_ref[:, v0 : v0 + vw]
        g = x_ref[:, g0 : g0 + vw]
        forget = fg_ref[head : head + 1, :]
        weight = decay(ig_ref[head : head + 1, :], forget, length, qk**-0.5)
        scores = dot(q, k, NT) * weight
        pulled = dot(g, v, NT)
        norm = jnp.sum(scores, axis=1, keepdims=True)
        along = jnp.sum(scores * pulled, axis=1, keepdims=True)
        size_of = jnp.abs(norm)
        inverse = 1.0 / jnp.maximum(size_of, 1.0)
        share = jnp.where(size_of > 1.0, 1.0, jnp.where(size_of == 1.0, 0.5, 0.0))
        grad_norm = -along * inverse * inverse * share * jnp.where(norm < 0.0, -1.0, 1.0)
        grad_scores = pulled * inverse + grad_norm
        hidden = wide_dot(scores * inverse, v, NN)
        grad_raw = grad_scores * weight
        gq = wide_dot(grad_raw, k, NN)
        gk = wide_dot(grad_raw.T, q, NN)
        gv = wide_dot((scores * inverse).T, g, NN)
        out_ref[:, head * qk : (head + 1) * qk] = gq.astype(jnp.bfloat16)
        out_ref[:, (heads + head) * qk : (heads + head + 1) * qk] = gk.astype(jnp.bfloat16)
        out_ref[:, v0 : v0 + vw] = gv.astype(jnp.bfloat16)
        out_ref[:, g0 : g0 + vw] = hidden.astype(jnp.bfloat16)
        by_column = jnp.sum(grad_scores * scores, axis=0, keepdims=True)
        by_row = along * inverse * (1.0 - share)
        moved = by_row - jnp.sum(jnp.where(rows == cols, by_column, 0.0), axis=1, keepdims=True)
        grad_log = jnp.sum(jnp.where(rows >= cols, moved, 0.0), axis=0, keepdims=True)
        gi_ref[head : head + 1, :] = by_column
        gf_ref[head : head + 1, :] = jnp.where(
            cols[:1] < length, grad_log / (1.0 + jnp.exp(forget)), 0.0
        )


def shards(queries, keys, values, cotangent, igate, fgate, lengths):
    devices = lax.axis_size("head")
    rows = queries.shape[0]
    heads = igate.shape[0]
    qk = queries.shape[1] // (devices * heads)
    vw = values.shape[1] // (devices * heads)
    parts = [a.reshape(rows, devices, -1) for a in (queries, keys, values, cotangent)]
    joined = jnp.concatenate(parts, axis=2)
    here = lax.all_to_all(joined, "head", split_axis=1, concat_axis=0, tiled=True)
    here = here.reshape(rows * devices, -1)
    vmem = pl.BlockSpec(memory_space=pltpu.VMEM)
    out, grad_in, grad_forget = pl.pallas_call(
        functools.partial(whole_kernel, heads, qk, vw),
        out_shape=(
            jax.ShapeDtypeStruct(here.shape, jnp.bfloat16),
            jax.ShapeDtypeStruct(igate.shape, jnp.float32),
            jax.ShapeDtypeStruct(igate.shape, jnp.float32),
        ),
        in_specs=[pl.BlockSpec(memory_space=pltpu.SMEM), vmem, vmem, vmem],
        out_specs=(vmem, vmem, vmem),
        compiler_params=pltpu.CompilerParams(vmem_limit_bytes=32 * 1024 * 1024),
    )(lengths, here, igate, fgate)
    back = lax.all_to_all(
        out.reshape(devices, rows, -1), "head", split_axis=0, concat_axis=0, tiled=True
    )
    back = back.transpose(1, 0, 2)
    ends = [0, heads * qk, 2 * heads * qk, 2 * heads * qk + heads * vw, back.shape[2]]
    gq, gk, gv, hidden = [
        back[:, :, a:b].reshape(rows, -1) for a, b in zip(ends[:-1], ends[1:])
    ]
    return hidden, gq, gk, gv, grad_in, grad_forget


def solution(mesh):
    rows = P(("groups", "seq", "head"), None)
    gates = P("head", ("groups", "seq"))
    return jax.shard_map(
        shards,
        mesh=mesh,
        in_specs=(rows, rows, rows, rows, gates, gates, P(("groups", "seq"))),
        out_specs=(rows, rows, rows, rows, gates, gates),
        check_vma=False,
    )
```

```python
import functools

import jax
import jax.numpy as jnp
from jax import lax
from jax.experimental import pallas as pl
from jax.experimental.pallas import tpu as pltpu
from jax.sharding import PartitionSpec as P

FAR = -1e30


def dot(left, right, contract):
    return lax.dot_general(left, right, (contract, ((), ())), preferred_element_type=jnp.float32)


def halves(value):
    high = value.astype(jnp.bfloat16)
    return high, (value - high.astype(jnp.float32)).astype(jnp.bfloat16)


def wide_dot(left, right, contract):
    high, low = halves(left)
    return dot(high, right, contract) + dot(low, right, contract)


NN = ((1,), (0,))
NT = ((1,), (1,))
TN = ((0,), (0,))


def log_sigmoid(value):
    return jnp.minimum(value, 0.0) - jnp.log(1.0 + jnp.exp(-jnp.abs(value)))


def decay(in_gate, forget_gate, length, scale):
    size = in_gate.shape[1]
    rows = lax.broadcasted_iota(jnp.int32, (size, size), 0)
    cols = lax.broadcasted_iota(jnp.int32, (size, size), 1)
    logs = jnp.where(cols[:1] < length, log_sigmoid(forget_gate), 0.0)
    total_col = jnp.sum(jnp.where(cols <= rows, logs, 0.0), axis=1, keepdims=True)
    total_row = jnp.sum(jnp.where(cols == rows, total_col, 0.0), axis=0, keepdims=True)
    mask = (cols <= rows) & (rows < length)
    return jnp.exp(jnp.where(mask, total_col - total_row, FAR)) * (jnp.exp(in_gate) * scale)


def whole_kernel(heads, qk, vw, length_ref, x_ref, ig_ref, fg_ref, out_ref, gi_ref, gf_ref):
    length = length_ref[0]
    size = x_ref.shape[0]
    rows = lax.broadcasted_iota(jnp.int32, (size, size), 0)
    cols = lax.broadcasted_iota(jnp.int32, (size, size), 1)
    for head in range(heads):
        q = x_ref[:, head * qk : (head + 1) * qk]
        k = x_ref[:, (heads + head) * qk : (heads + head + 1) * qk]
        v0 = 2 * heads * qk + head * vw
        g0 = v0 + heads * vw
        v = x_ref[:, v0 : v0 + vw]
        g = x_ref[:, g0 : g0 + vw]
        forget = fg_ref[head : head + 1, :]
        weight = decay(ig_ref[head : head + 1, :], forget, length, qk**-0.5)
        scores = dot(q, k, NT) * weight
        pulled = dot(g, v, NT)
        norm = jnp.sum(scores, axis=1, keepdims=True)
        along = jnp.sum(scores * pulled, axis=1, keepdims=True)
        size_of = jnp.abs(norm)
        inverse = 1.0 / jnp.maximum(size_of, 1.0)
        share = jnp.where(size_of > 1.0, 1.0, jnp.where(size_of == 1.0, 0.5, 0.0))
        grad_norm = -along * inverse * inverse * share * jnp.where(norm < 0.0, -1.0, 1.0)
        grad_scores = pulled * inverse + grad_norm
        hidden = wide_dot(scores * inverse, v, NN)
        grad_raw = grad_scores * weight
        gq = wide_dot(grad_raw, k, NN)
        gk = wide_dot(grad_raw.T, q, NN)
        gv = wide_dot((scores * inverse).T, g, NN)
        out_ref[:, head * qk : (head + 1) * qk] = gq.astype(jnp.bfloat16)
        out_ref[:, (heads + head) * qk : (heads + head + 1) * qk] = gk.astype(jnp.bfloat16)
        out_ref[:, v0 : v0 + vw] = gv.astype(jnp.bfloat16)
        out_ref[:, g0 : g0 + vw] = hidden.astype(jnp.bfloat16)
        by_column = jnp.sum(grad_scores * scores, axis=0, keepdims=True)
        by_row = along * inverse * (1.0 - share)
        moved = by_row - jnp.sum(jnp.where(rows == cols, by_column, 0.0), axis=1, keepdims=True)
        grad_log = jnp.sum(jnp.where(rows >= cols, moved, 0.0), axis=0, keepdims=True)
        gi_ref[head : head + 1, :] = by_column
        gf_ref[head : head + 1, :] = jnp.where(
            cols[:1] < length, grad_log / (1.0 + jnp.exp(forget)), 0.0
        )


def swapped_shards(queries, keys, values, cotangent, igate, fgate, lengths):
    devices = lax.axis_size("head")
    rows = queries.shape[0]
    heads = igate.shape[0]
    qk = queries.shape[1] // (devices * heads)
    vw = values.shape[1] // (devices * heads)
    parts = [a.reshape(rows, devices, -1) for a in (queries, keys, values, cotangent)]
    joined = jnp.concatenate(parts, axis=2)
    here = lax.all_to_all(joined, "head", split_axis=1, concat_axis=0, tiled=True)
    here = here.reshape(rows * devices, -1)
    vmem = pl.BlockSpec(memory_space=pltpu.VMEM)
    out, grad_in, grad_forget = pl.pallas_call(
        functools.partial(whole_kernel, heads, qk, vw),
        out_shape=(
            jax.ShapeDtypeStruct(here.shape, jnp.bfloat16),
            jax.ShapeDtypeStruct(igate.shape, jnp.float32),
            jax.ShapeDtypeStruct(igate.shape, jnp.float32),
        ),
        in_specs=[pl.BlockSpec(memory_space=pltpu.SMEM), vmem, vmem, vmem],
        out_specs=(vmem, vmem, vmem),
        compiler_params=pltpu.CompilerParams(vmem_limit_bytes=32 * 1024 * 1024),
    )(lengths, here, igate, fgate)
    back = lax.all_to_all(
        out.reshape(devices, rows, -1), "head", split_axis=0, concat_axis=0, tiled=True
    )
    back = back.transpose(1, 0, 2)
    ends = [0, heads * qk, 2 * heads * qk, 2 * heads * qk + heads * vw, back.shape[2]]
    gq, gk, gv, hidden = [
        back[:, :, a:b].reshape(rows, -1) for a, b in zip(ends[:-1], ends[1:])
    ]
    return hidden, gq, gk, gv, grad_in, grad_forget


def backward_terms(norm, along):
    size = jnp.abs(norm)
    inverse = 1.0 / jnp.maximum(size, 1.0)
    share = jnp.where(size > 1.0, 1.0, jnp.where(size == 1.0, 0.5, 0.0))
    grad_norm = -along * inverse * inverse * share * jnp.where(norm < 0.0, -1.0, 1.0)
    return inverse, grad_norm, along * inverse * (1.0 - share)


def place():
    me = lax.axis_index("head")
    return me // 2, lax.rem(me, 2)


def run_copies(pairs, sems):
    copies = [pltpu.make_async_copy(a, b, sems.at[i]) for i, (a, b) in enumerate(pairs)]
    for copy in copies:
        copy.start()
    return copies


def pack_kernel(q_ref, k_ref, v_ref, g_ref, ig_ref, fg_ref, m1_ref, a2_ref, a3_ref, b2_ref, b3_ref, gates_ref, sems):
    chip, core = place()
    wq, wv = q_ref.shape[1] // 4, v_ref.shape[1] // 4
    heads = ig_ref.shape[0]

    def block(ref, owner, width):
        return ref.at[:, pl.ds(pl.multiple_of(owner * width, width), width)]

    def cross(first, second):
        pairs = []
        for chunk, (same, other) in enumerate(((a2_ref, a3_ref), (b2_ref, b3_ref))):
            for target, to in ((same, core), (other, 1 - core)):
                pairs.append((block(first, 2 * chunk + to, wq), target.at[:, :wq]))
                pairs.append((block(second, 2 * chunk + to, wv), target.at[:, wq:]))
        return pairs

    @pl.when(chip == 0)
    def _():
        run_copies(cross(k_ref, v_ref), sems)

    @pl.when(chip != 0)
    def _():
        run_copies(cross(q_ref, g_ref), sems)

    pairs = []
    for chunk in range(2):
        start = chunk * 2 * (wq + wv)
        for ref, width in ((q_ref, wq), (g_ref, wv), (k_ref, wq), (v_ref, wv)):
            pairs.append((block(ref, 2 * chunk + 1 - core, width), m1_ref.at[:, start : start + width]))
            start += width
    copies = run_copies(pairs, sems.at[pl.ds(8, 8)])
    gates_ref[:heads, :] = ig_ref[...]
    gates_ref[heads:, :] = fg_ref[...]
    for i, (source, target) in enumerate(cross(k_ref, v_ref)):
        pltpu.make_async_copy(source, target, sems.at[i]).wait()
    for copy in copies:
        copy.wait()


def local_kernel(qk, vw, length_ref, q_ref, k_ref, v_ref, g_ref, m1_ref, own_ref, got_ref, qg_ref, kv_ref, stats_ref, sems):
    chip, core = place()
    rows = q_ref.shape[0]
    heads = own_ref.shape[0] // 2
    wq, wv = heads * qk, heads * vw
    pairs = []
    mine = pl.ds(pl.multiple_of(core * rows, rows), rows)
    theirs = pl.ds(pl.multiple_of((1 - core) * rows, rows), rows)
    for chunk in range(2):
        start = chunk * 2 * (wq + wv)
        owner = 2 * chunk + core
        for first, second, target in ((q_ref, g_ref, qg_ref), (k_ref, v_ref, kv_ref)):
            pairs.append((first.at[:, pl.ds(pl.multiple_of(owner * wq, wq), wq)], target.at[chunk, mine, :wq]))
            pairs.append((second.at[:, pl.ds(pl.multiple_of(owner * wv, wv), wv)], target.at[chunk, mine, wq:]))
            pairs.append((m1_ref.at[:, start : start + wq + wv], target.at[chunk, theirs, :]))
            start += wq + wv
    copies = run_copies(pairs, sems)
    stats_ref[...] = jnp.zeros_like(stats_ref)
    for copy in copies:
        copy.wait()
    length = length_ref[0]

    def part(side, chunk):
        gates = own_ref if side == chunk else got_ref
        size = 2 * rows
        low = side * size
        for head in range(heads):
            q = qg_ref[chunk, :, head * qk : (head + 1) * qk]
            k = kv_ref[chunk, :, head * qk : (head + 1) * qk]
            g = qg_ref[chunk, :, wq + head * vw : wq + (head + 1) * vw]
            v = kv_ref[chunk, :, wq + head * vw : wq + (head + 1) * vw]
            weight = decay(gates[head : head + 1, :], gates[heads + head : heads + head + 1, :], length, qk**-0.5)
            weight = weight[low : low + size, low : low + size]
            scores = dot(q, k, NT) * weight
            pulled = dot(g, v, NT)
            norm = jnp.sum(scores, axis=1, keepdims=True)
            along = jnp.sum(scores * pulled, axis=1, keepdims=True)
            on = lax.broadcasted_iota(jnp.int32, (size, 2 * size), 0) + low == lax.broadcasted_iota(
                jnp.int32, (size, 2 * size), 1
            )

            def as_row(column):
                return jnp.sum(jnp.where(on, column, 0.0), axis=0, keepdims=True)

            if side == 1:
                at = chunk * heads + head
                stats_ref[at : at + 1, :] = as_row(norm)
                stats_ref[2 * heads + at : 2 * heads + at + 1, :] = as_row(along)
            else:
                inverse, grad_norm, by_row = backward_terms(norm, along)
                by_column = jnp.sum((pulled * inverse + grad_norm) * scores, axis=0, keepdims=True)
                stats_ref[head : head + 1, :size] = by_column
                stats_ref[heads + head : heads + head + 1, :] = as_row(by_row)

    @pl.when(chip == 0)
    def _():
        part(0, 1)

    @pl.when(chip != 0)
    def _():
        part(1, 0)
        part(1, 1)


def cross_kernel(
    chunk, qk, vw, length_ref, qg_ref, kv_ref, same_ref, other_ref, own_ref, got_ref, stats_ref,
    mine_ref, theirs_ref, gates_ref, wide_ref, thin_ref, result_ref, sems,
):
    chip, core = place()
    rows = same_ref.shape[0]
    size = 2 * rows
    heads = own_ref.shape[0] // 2
    wq, wv = heads * qk, heads * vw

    def gather(side, wide, thin):
        base = 0 if side else size
        at_same = pl.ds(pl.multiple_of(base + core * rows, rows), rows)
        at_other = pl.ds(pl.multiple_of(base + (1 - core) * rows, rows), rows)
        local = wide_ref.at[side * size : (side + 1) * size, :]
        return [
            (wide.at[chunk], local),
            (thin.at[chunk], thin_ref),
            (same_ref, wide_ref.at[at_same, :]),
            (other_ref, wide_ref.at[at_other, :]),
        ]

    length = length_ref[0]
    gates_ref[...] = jnp.zeros_like(gates_ref)

    def part(side):
        copies = run_copies(gather(side, *((kv_ref, qg_ref) if side else (qg_ref, kv_ref))), sems)
        gates = own_ref if side == chunk else got_ref
        full = 2 * size
        rows_at = lax.broadcasted_iota(jnp.int32, (full, full), 0)
        cols_at = lax.broadcasted_iota(jnp.int32, (full, full), 1)

        def as_column(row):
            return jnp.sum(jnp.where(rows_at == cols_at, row, 0.0), axis=1, keepdims=True)

        weights = [
            decay(gates[head : head + 1, :], gates[heads + head : heads + head + 1, :], length, qk**-0.5)
            for head in range(heads)
        ]
        for copy in copies:
            copy.wait()
        for head in range(heads):
            first = slice(head * qk, (head + 1) * qk)
            second = slice(wq + head * vw, wq + (head + 1) * vw)
            if side == 0:
                q, g, k, v = wide_ref[:, first], wide_ref[:, second], thin_ref[:, first], thin_ref[:, second]
                weight = weights[head][:, :size]
            else:
                k, v, q, g = wide_ref[:, first], wide_ref[:, second], thin_ref[:, first], thin_ref[:, second]
                weight = weights[head][size:, :]
            scores = dot(q, k, NT) * weight
            pulled = dot(g, v, NT)
            norm = jnp.sum(scores, axis=1, keepdims=True)
            along = jnp.sum(scores * pulled, axis=1, keepdims=True)
            if side == 0:
                at = chunk * heads + head
                norm = norm + as_column(stats_ref[at : at + 1, :])
                along = along + as_column(stats_ref[2 * heads + at : 2 * heads + at + 1, :])
            inverse, grad_norm, by_row = backward_terms(norm, along)
            grad_scores = pulled * inverse + grad_norm
            scaled = scores * inverse
            grad_raw = grad_scores * weight
            if side == 0:
                hidden = wide_dot(scaled[:size], v, NN)
                gq = wide_dot(grad_raw[:size], k, NN)
                gk = wide_dot(grad_raw.T, q, NN)
                gv = wide_dot(scaled.T, g, NN)
            else:
                hidden = wide_dot(scaled, v, NN)
                gq = wide_dot(grad_raw, k, NN)
                gk = wide_dot(grad_raw.T[size:], q, NN)
                gv = wide_dot(scaled.T[size:], g, NN)
            result_ref[:, head * qk : (head + 1) * qk] = gq.astype(jnp.bfloat16)
            result_ref[:, wq + head * qk : wq + (head + 1) * qk] = gk.astype(jnp.bfloat16)
            result_ref[:, 2 * wq + head * vw : 2 * wq + (head + 1) * vw] = gv.astype(jnp.bfloat16)
            result_ref[:, 2 * wq + wv + head * vw : 2 * wq + wv + (head + 1) * vw] = hidden.astype(jnp.bfloat16)
            by_column = jnp.sum(grad_scores * scores, axis=0, keepdims=True)
            forget = gates[heads + head : heads + head + 1, :]
            live = cols_at[:1] < length
            slope = jnp.where(live, 1.0 / (1.0 + jnp.exp(forget)), 0.0)
            if side == 0 and chunk == 0:
                small_rows, small_cols = rows_at[:size, :size], cols_at[:size, :size]
                column = jnp.sum(jnp.where(small_rows == small_cols, by_column, 0.0), axis=1, keepdims=True)
                before = jnp.where(small_rows < small_cols, column - by_row[:size], 0.0)
                grad_log = jnp.sum(before, axis=0, keepdims=True)
                gates_ref[head : head + 1, :size] = by_column
                gates_ref[heads + head : heads + head + 1, :size] = grad_log * slope[:, :size]
            if side == 1:
                row = jnp.sum(jnp.where(rows_at[size:] == cols_at[size:], by_row, 0.0), axis=0, keepdims=True)
                if chunk == 1:
                    by_column = by_column + stats_ref[head : head + 1, :]
                    row = row + stats_ref[heads + head : heads + head + 1, :]
                    seen = jnp.full((1, full), True)
                else:
                    seen = cols_at[:1] >= size
                by_column = jnp.where(seen, by_column, 0.0)
                moved = as_column(row - by_column)
                grad_log = jnp.sum(jnp.where(rows_at >= cols_at, moved, 0.0), axis=0, keepdims=True)
                gates_ref[head : head + 1, :] = by_column
                gates_ref[heads + head : heads + head + 1, :] = jnp.where(seen, grad_log * slope, 0.0)
        out = run_copies(
            [
                (result_ref.at[pl.ds(pl.multiple_of(core * rows, rows), rows), :], mine_ref),
                (result_ref.at[pl.ds(pl.multiple_of((1 - core) * rows, rows), rows), :], theirs_ref),
            ],
            sems.at[pl.ds(4, 2)],
        )
        for copy in out:
            copy.wait()

    @pl.when(chip == 0)
    def _():
        part(0)

    @pl.when(chip != 0)
    def _():
        part(1)


def merge_kernel(
    mine_a, mine_b, got_a, got_b, gates_a, gates_got, gates_b, hidden_ref, gq_ref, gk_ref, gv_ref, gi_ref, gf_ref, sems
):
    chip, core = place()
    heads = gi_ref.shape[0]
    wq, wv = gq_ref.shape[1] // 4, gv_ref.shape[1] // 4
    pairs = []
    for chunk, sources in enumerate(((mine_a, got_a), (mine_b, got_b))):
        for source, by in zip(sources, (core, 1 - core)):
            start = 0
            for target, width in ((gq_ref, wq), (gk_ref, wq), (gv_ref, wv), (hidden_ref, wv)):
                at = pl.ds(pl.multiple_of((2 * chunk + by) * width, width), width)
                pairs.append((source.at[:, start : start + width], target.at[:, at]))
                start += width
    copies = run_copies(pairs, sems)
    gates = jnp.where(chip == 0, gates_a[...] + gates_got[...], gates_b[...])
    gi_ref[...] = gates[:heads]
    gf_ref[...] = gates[heads:]
    for copy in copies:
        copy.wait()


def split_shards(queries, keys, values, cotangent, igate, fgate, lengths):
    rows = queries.shape[0]
    heads = igate.shape[0]
    qk = queries.shape[1] // (4 * heads)
    vw = values.shape[1] // (4 * heads)
    width = heads * (qk + vw)
    bf16, f32 = jnp.bfloat16, jnp.float32
    shape = jax.ShapeDtypeStruct
    vmem = pl.BlockSpec(memory_space=pltpu.VMEM)
    smem = pl.BlockSpec(memory_space=pltpu.SMEM)
    hbm = pl.BlockSpec(memory_space=pl.ANY)
    params = pltpu.CompilerParams(vmem_limit_bytes=32 * 1024 * 1024)
    dma = pltpu.SemaphoreType.DMA

    def swap(value, mask):
        return lax.ppermute(value, "head", [(s, s ^ mask) for s in range(4)])

    cross_shape = shape((rows, width), bf16)
    to_core, a2, a3, b2, b3, gates = pl.pallas_call(
        pack_kernel,
        out_shape=(shape((rows, 4 * width), bf16),) + (cross_shape,) * 4 + (shape((2 * heads, igate.shape[1]), f32),),
        in_specs=[hbm] * 4 + [vmem] * 2,
        out_specs=(hbm,) * 5 + (vmem,),
        scratch_shapes=[dma((16,))],
        compiler_params=params,
    )(queries, keys, values, cotangent, igate, fgate)
    gates_got = swap(gates, 2)
    a2, a3 = swap(a2, 2), swap(a3, 3)
    from_core = swap(to_core, 1)
    b2, b3 = swap(b2, 2), swap(b3, 3)
    both = shape((2, 2 * rows, width), bf16)
    stats_shape = shape((4 * heads, igate.shape[1]), f32)
    qg, kv, stats = pl.pallas_call(
        functools.partial(local_kernel, qk, vw),
        out_shape=(both, both, stats_shape),
        in_specs=[smem] + [hbm] * 5 + [vmem] * 2,
        out_specs=(vmem,) * 3,
        scratch_shapes=[dma((12,))],
        compiler_params=params,
    )(lengths, queries, keys, values, cotangent, from_core, gates, gates_got)
    stats = swap(stats, 2)

    def cross(chunk, same, other):
        out_shape = shape((rows, 2 * width), bf16)
        return pl.pallas_call(
            functools.partial(cross_kernel, chunk, qk, vw),
            out_shape=(out_shape, out_shape, shape(gates.shape, f32)),
            in_specs=[smem] + [hbm] * 4 + [vmem] * 3,
            out_specs=(hbm, hbm, vmem),
            scratch_shapes=[
                pltpu.VMEM((4 * rows, width), bf16),
                pltpu.VMEM((2 * rows, width), bf16),
                pltpu.VMEM((2 * rows, 2 * width), bf16),
                dma((6,)),
            ],
            compiler_params=params,
        )(lengths, qg, kv, same, other, gates, gates_got, stats)

    mine_a, theirs_a, gates_a = cross(0, a2, a3)
    gates_back = swap(gates_a, 2)
    got_a = swap(theirs_a, 1)
    mine_b, theirs_b, gates_b = cross(1, b2, b3)
    got_b = swap(theirs_b, 1)
    gate_shape = shape(igate.shape, f32)
    return pl.pallas_call(
        merge_kernel,
        out_shape=(
            shape(values.shape, bf16), shape(queries.shape, bf16), shape(keys.shape, bf16), shape(values.shape, bf16),
            gate_shape, gate_shape,
        ),
        in_specs=[hbm] * 4 + [vmem] * 3,
        out_specs=(hbm,) * 4 + (vmem,) * 2,
        scratch_shapes=[dma((16,))],
        compiler_params=params,
    )(mine_a, mine_b, got_a, got_b, gates_a, gates_back, gates_b)


def shards(*arrays):
    if lax.axis_size("head") == 4:
        return split_shards(*arrays)
    return swapped_shards(*arrays)


def solution(mesh):
    rows = P(("groups", "seq", "head"), None)
    gates = P("head", ("groups", "seq"))
    return jax.shard_map(
        shards,
        mesh=mesh,
        in_specs=(rows, rows, rows, rows, gates, gates, P(("groups", "seq"))),
        out_specs=(rows, rows, rows, rows, gates, gates),
        check_vma=False,
    )
```

```python
import functools

import jax
import jax.numpy as jnp
from jax import lax
from jax.experimental import pallas as pl
from jax.experimental.pallas import tpu as pltpu
from jax.sharding import PartitionSpec as P

FAR = -1e30


def dot(left, right, contract):
    return lax.dot_general(left, right, (contract, ((), ())), preferred_element_type=jnp.float32)


def halves(value):
    high = value.astype(jnp.bfloat16)
    return high, (value - high.astype(jnp.float32)).astype(jnp.bfloat16)


def wide_dot(left, right, contract):
    rows = left.shape[0]
    both = dot(jnp.concatenate(halves(left), axis=0), right, contract)
    return both[:rows] + both[rows:]


NN = ((1,), (0,))
NT = ((1,), (1,))
TN = ((0,), (0,))


def log_sigmoid(value):
    return jnp.minimum(value, 0.0) - jnp.log(1.0 + jnp.exp(-jnp.abs(value)))


def decay(in_gate, forget_gate, length, scale):
    size = in_gate.shape[1]
    rows = lax.broadcasted_iota(jnp.int32, (size, size), 0)
    cols = lax.broadcasted_iota(jnp.int32, (size, size), 1)
    logs = jnp.where(cols[:1] < length, log_sigmoid(forget_gate), 0.0)
    total_col = jnp.sum(jnp.where(cols <= rows, logs, 0.0), axis=1, keepdims=True)
    total_row = jnp.sum(jnp.where(cols == rows, total_col, 0.0), axis=0, keepdims=True)
    mask = (cols <= rows) & (rows < length)
    return jnp.exp(jnp.where(mask, total_col - total_row, FAR)) * (jnp.exp(in_gate) * scale)


def whole_kernel(heads, qk, vw, length_ref, x_ref, ig_ref, fg_ref, out_ref, gi_ref, gf_ref):
    length = length_ref[0]
    size = x_ref.shape[0]
    rows = lax.broadcasted_iota(jnp.int32, (size, size), 0)
    cols = lax.broadcasted_iota(jnp.int32, (size, size), 1)
    for head in range(heads):
        q = x_ref[:, head * qk : (head + 1) * qk]
        k = x_ref[:, (heads + head) * qk : (heads + head + 1) * qk]
        v0 = 2 * heads * qk + head * vw
        g0 = v0 + heads * vw
        v = x_ref[:, v0 : v0 + vw]
        g = x_ref[:, g0 : g0 + vw]
        forget = fg_ref[head : head + 1, :]
        weight = decay(ig_ref[head : head + 1, :], forget, length, qk**-0.5)
        scores = dot(q, k, NT) * weight
        pulled = dot(g, v, NT)
        norm = jnp.sum(scores, axis=1, keepdims=True)
        along = jnp.sum(scores * pulled, axis=1, keepdims=True)
        size_of = jnp.abs(norm)
        inverse = 1.0 / jnp.maximum(size_of, 1.0)
        share = jnp.where(size_of > 1.0, 1.0, jnp.where(size_of == 1.0, 0.5, 0.0))
        grad_norm = -along * inverse * inverse * share * jnp.where(norm < 0.0, -1.0, 1.0)
        grad_scores = pulled * inverse + grad_norm
        hidden = wide_dot(scores * inverse, v, NN)
        grad_raw = grad_scores * weight
        gq = wide_dot(grad_raw, k, NN)
        gk = wide_dot(grad_raw.T, q, NN)
        gv = wide_dot((scores * inverse).T, g, NN)
        out_ref[:, head * qk : (head + 1) * qk] = gq.astype(jnp.bfloat16)
        out_ref[:, (heads + head) * qk : (heads + head + 1) * qk] = gk.astype(jnp.bfloat16)
        out_ref[:, v0 : v0 + vw] = gv.astype(jnp.bfloat16)
        out_ref[:, g0 : g0 + vw] = hidden.astype(jnp.bfloat16)
        by_column = jnp.sum(grad_scores * scores, axis=0, keepdims=True)
        by_row = along * inverse * (1.0 - share)
        moved = by_row - jnp.sum(jnp.where(rows == cols, by_column, 0.0), axis=1, keepdims=True)
        grad_log = jnp.sum(jnp.where(rows >= cols, moved, 0.0), axis=0, keepdims=True)
        gi_ref[head : head + 1, :] = by_column
        gf_ref[head : head + 1, :] = jnp.where(
            cols[:1] < length, grad_log / (1.0 + jnp.exp(forget)), 0.0
        )


def swapped_shards(queries, keys, values, cotangent, igate, fgate, lengths):
    devices = lax.axis_size("head")
    rows = queries.shape[0]
    heads = igate.shape[0]
    qk = queries.shape[1] // (devices * heads)
    vw = values.shape[1] // (devices * heads)
    parts = [a.reshape(rows, devices, -1) for a in (queries, keys, values, cotangent)]
    joined = jnp.concatenate(parts, axis=2)
    here = lax.all_to_all(joined, "head", split_axis=1, concat_axis=0, tiled=True)
    here = here.reshape(rows * devices, -1)
    vmem = pl.BlockSpec(memory_space=pltpu.VMEM)
    out, grad_in, grad_forget = pl.pallas_call(
        functools.partial(whole_kernel, heads, qk, vw),
        out_shape=(
            jax.ShapeDtypeStruct(here.shape, jnp.bfloat16),
            jax.ShapeDtypeStruct(igate.shape, jnp.float32),
            jax.ShapeDtypeStruct(igate.shape, jnp.float32),
        ),
        in_specs=[pl.BlockSpec(memory_space=pltpu.SMEM), vmem, vmem, vmem],
        out_specs=(vmem, vmem, vmem),
        compiler_params=pltpu.CompilerParams(vmem_limit_bytes=32 * 1024 * 1024),
    )(lengths, here, igate, fgate)
    back = lax.all_to_all(
        out.reshape(devices, rows, -1), "head", split_axis=0, concat_axis=0, tiled=True
    )
    back = back.transpose(1, 0, 2)
    ends = [0, heads * qk, 2 * heads * qk, 2 * heads * qk + heads * vw, back.shape[2]]
    gq, gk, gv, hidden = [
        back[:, :, a:b].reshape(rows, -1) for a, b in zip(ends[:-1], ends[1:])
    ]
    return hidden, gq, gk, gv, grad_in, grad_forget


def backward_terms(norm, along):
    size = jnp.abs(norm)
    inverse = 1.0 / jnp.maximum(size, 1.0)
    share = jnp.where(size > 1.0, 1.0, jnp.where(size == 1.0, 0.5, 0.0))
    grad_norm = -along * inverse * inverse * share * jnp.where(norm < 0.0, -1.0, 1.0)
    return inverse, grad_norm, along * inverse * (1.0 - share)


def place():
    me = lax.axis_index("head")
    return me // 2, lax.rem(me, 2)


def run_copies(pairs, sems):
    copies = [pltpu.make_async_copy(a, b, sems.at[i]) for i, (a, b) in enumerate(pairs)]
    for copy in copies:
        copy.start()
    return copies


def pack_kernel(
    q_ref, k_ref, v_ref, g_ref, ig_ref, fg_ref, m1_ref, a2_ref, a3_ref, qg_ref, kv_ref, gates_ref, in_ref, out_ref, sems
):
    chip, core = place()
    wq, wv = q_ref.shape[1] // 4, v_ref.shape[1] // 4
    heads = ig_ref.shape[0]

    def block(ref, owner, width):
        return ref.at[:, pl.ds(pl.multiple_of(owner * width, width), width)]

    def cross(first, second):
        pairs = []
        for target, to in ((a2_ref, core), (a3_ref, 1 - core)):
            pairs.append((block(first, to, wq), target.at[:, :wq]))
            pairs.append((block(second, to, wv), target.at[:, wq:]))
        return pairs

    @pl.when(chip == 0)
    def _():
        run_copies(cross(k_ref, v_ref), sems)

    @pl.when(chip != 0)
    def _():
        run_copies(cross(q_ref, g_ref), sems)

    pairs = [(ig_ref, in_ref), (fg_ref, out_ref)]
    for chunk in range(2):
        start = chunk * 2 * (wq + wv)
        for first, second, own in ((q_ref, g_ref, qg_ref), (k_ref, v_ref, kv_ref)):
            for ref, width, at in ((first, wq, slice(0, wq)), (second, wv, slice(wq, wq + wv))):
                pairs.append((block(ref, 2 * chunk + 1 - core, width), m1_ref.at[:, start : start + width]))
                pairs.append((block(ref, 2 * chunk + core, width), own.at[chunk, :, at]))
                start += width
    copies = run_copies(pairs, sems.at[pl.ds(4, 18)])
    for copy in copies[:2]:
        copy.wait()
    gates_ref[:heads, :] = in_ref[...]
    gates_ref[heads:, :] = out_ref[...]
    for i, (source, target) in enumerate(cross(k_ref, v_ref)):
        pltpu.make_async_copy(source, target, sems.at[i]).wait()
    for copy in copies[2:]:
        copy.wait()


def local_kernel(qk, vw, length_ref, own_qg, own_kv, m1_ref, own_ref, got_ref, qg_ref, kv_ref, send_ref, stats_ref):
    chip, core = place()
    rows = m1_ref.shape[0]
    heads = own_ref.shape[0] // 2
    wq, wv = heads * qk, heads * vw
    width = wq + wv
    mine = pl.ds(pl.multiple_of(core * rows, rows), rows)
    theirs = pl.ds(pl.multiple_of((1 - core) * rows, rows), rows)
    for chunk in range(2):
        start = chunk * 2 * width
        qg_ref[chunk, mine, :] = own_qg[chunk]
        qg_ref[chunk, theirs, :] = m1_ref[:, start : start + width]
        kv_ref[chunk, mine, :] = own_kv[chunk]
        kv_ref[chunk, theirs, :] = m1_ref[:, start + width : start + 2 * width]
    stats_ref[...] = jnp.zeros_like(stats_ref)
    length = length_ref[0]

    def part(side, chunk):
        gates = own_ref if side == chunk else got_ref
        size = 2 * rows
        low = side * size
        for head in range(heads):
            q = qg_ref[chunk, :, head * qk : (head + 1) * qk]
            k = kv_ref[chunk, :, head * qk : (head + 1) * qk]
            g = qg_ref[chunk, :, wq + head * vw : wq + (head + 1) * vw]
            v = kv_ref[chunk, :, wq + head * vw : wq + (head + 1) * vw]
            weight = decay(gates[head : head + 1, :], gates[heads + head : heads + head + 1, :], length, qk**-0.5)
            weight = weight[low : low + size, low : low + size]
            scores = dot(q, k, NT) * weight
            pulled = dot(g, v, NT)
            norm = jnp.sum(scores, axis=1, keepdims=True)
            along = jnp.sum(scores * pulled, axis=1, keepdims=True)
            on = lax.broadcasted_iota(jnp.int32, (size, 2 * size), 0) + low == lax.broadcasted_iota(
                jnp.int32, (size, 2 * size), 1
            )

            def as_row(column):
                return jnp.sum(jnp.where(on, column, 0.0), axis=0, keepdims=True)

            if side == 1:
                at = chunk * heads + head
                stats_ref[at : at + 1, :] = as_row(norm)
                stats_ref[2 * heads + at : 2 * heads + at + 1, :] = as_row(along)
            else:
                inverse, grad_norm, by_row = backward_terms(norm, along)
                by_column = jnp.sum((pulled * inverse + grad_norm) * scores, axis=0, keepdims=True)
                stats_ref[head : head + 1, :size] = by_column
                stats_ref[heads + head : heads + head + 1, :] = as_row(by_row)

    @pl.when(chip == 0)
    def _():
        send_ref[...] = kv_ref[1]
        part(0, 1)

    @pl.when(chip != 0)
    def _():
        send_ref[...] = qg_ref[1]
        part(1, 0)
        part(1, 1)


def cross_kernel(
    chunk, qk, vw, length_ref, qg_ref, kv_ref, own_ref, got_ref, stats_ref, *refs
):
    *cross_refs, result_ref, theirs_ref, gates_ref, wide_ref = refs
    chip, core = place()
    rows = theirs_ref.shape[0]
    size = 2 * rows
    heads = own_ref.shape[0] // 2
    wq, wv = heads * qk, heads * vw

    def gather(side, local):
        base = 0 if side else size
        wide_ref[side * size : (side + 1) * size, :] = local[chunk]
        if len(cross_refs) == 1:
            wide_ref[base : base + size, :] = cross_refs[0][...]
        else:
            for ref, by in zip(cross_refs, (core, 1 - core)):
                wide_ref[pl.ds(pl.multiple_of(base + by * rows, rows), rows), :] = ref[...]

    length = length_ref[0]
    gates_ref[...] = jnp.zeros_like(gates_ref)

    def part(side):
        gather(side, kv_ref if side else qg_ref)
        thin = (qg_ref if side else kv_ref).at[chunk]
        gates = own_ref if side == chunk else got_ref
        full = 2 * size
        rows_at = lax.broadcasted_iota(jnp.int32, (full, full), 0)
        cols_at = lax.broadcasted_iota(jnp.int32, (full, full), 1)

        def as_column(row):
            return jnp.sum(jnp.where(rows_at == cols_at, row, 0.0), axis=1, keepdims=True)

        weights = [
            decay(gates[head : head + 1, :], gates[heads + head : heads + head + 1, :], length, qk**-0.5)
            for head in range(heads)
        ]
        for head in range(heads):
            first = slice(head * qk, (head + 1) * qk)
            second = slice(wq + head * vw, wq + (head + 1) * vw)
            if side == 0:
                q, g, k, v = wide_ref[:, first], wide_ref[:, second], thin[:, first], thin[:, second]
                weight = weights[head][:, :size]
            else:
                k, v, q, g = wide_ref[:, first], wide_ref[:, second], thin[:, first], thin[:, second]
                weight = weights[head][size:, :]
            scores = dot(q, k, NT) * weight
            pulled = dot(g, v, NT)
            norm = jnp.sum(scores, axis=1, keepdims=True)
            along = jnp.sum(scores * pulled, axis=1, keepdims=True)
            if side == 0:
                at = chunk * heads + head
                norm = norm + as_column(stats_ref[at : at + 1, :])
                along = along + as_column(stats_ref[2 * heads + at : 2 * heads + at + 1, :])
            inverse, grad_norm, by_row = backward_terms(norm, along)
            grad_scores = pulled * inverse + grad_norm
            scaled = scores * inverse
            grad_raw = grad_scores * weight
            if side == 0:
                hidden = wide_dot(scaled[:size], v, NN)
                gq = wide_dot(grad_raw[:size], k, NN)
                gk = wide_dot(grad_raw.T, q, NN)
                gv = wide_dot(scaled.T, g, NN)
            else:
                hidden = wide_dot(scaled, v, NN)
                gq = wide_dot(grad_raw, k, NN)
                gk = wide_dot(grad_raw.T[size:], q, NN)
                gv = wide_dot(scaled.T[size:], g, NN)
            result_ref[:, head * qk : (head + 1) * qk] = gq.astype(jnp.bfloat16)
            result_ref[:, wq + head * qk : wq + (head + 1) * qk] = gk.astype(jnp.bfloat16)
            result_ref[:, 2 * wq + head * vw : 2 * wq + (head + 1) * vw] = gv.astype(jnp.bfloat16)
            result_ref[:, 2 * wq + wv + head * vw : 2 * wq + wv + (head + 1) * vw] = hidden.astype(jnp.bfloat16)
            by_column = jnp.sum(grad_scores * scores, axis=0, keepdims=True)
            forget = gates[heads + head : heads + head + 1, :]
            live = cols_at[:1] < length
            slope = jnp.where(live, 1.0 / (1.0 + jnp.exp(forget)), 0.0)
            if side == 0 and chunk == 0:
                small_rows, small_cols = rows_at[:size, :size], cols_at[:size, :size]
                column = jnp.sum(jnp.where(small_rows == small_cols, by_column, 0.0), axis=1, keepdims=True)
                before = jnp.where(small_rows < small_cols, column - by_row[:size], 0.0)
                grad_log = jnp.sum(before, axis=0, keepdims=True)
                gates_ref[head : head + 1, :size] = by_column
                gates_ref[heads + head : heads + head + 1, :size] = grad_log * slope[:, :size]
            if side == 1:
                row = jnp.sum(jnp.where(rows_at[size:] == cols_at[size:], by_row, 0.0), axis=0, keepdims=True)
                if chunk == 1:
                    by_column = by_column + stats_ref[head : head + 1, :]
                    row = row + stats_ref[heads + head : heads + head + 1, :]
                    seen = jnp.full((1, full), True)
                else:
                    seen = cols_at[:1] >= size
                by_column = jnp.where(seen, by_column, 0.0)
                moved = as_column(row - by_column)
                grad_log = jnp.sum(jnp.where(rows_at >= cols_at, moved, 0.0), axis=0, keepdims=True)
                gates_ref[head : head + 1, :] = by_column
                gates_ref[heads + head : heads + head + 1, :] = jnp.where(seen, grad_log * slope, 0.0)
        theirs_ref[...] = result_ref[pl.ds(pl.multiple_of((1 - core) * rows, rows), rows), :]

    @pl.when(chip == 0)
    def _():
        part(0)

    @pl.when(chip != 0)
    def _():
        part(1)


def placed(source, targets, chunk, by):
    pairs = []
    start = 0
    for target in targets:
        width = target.shape[1] // 4
        at = pl.ds(pl.multiple_of((2 * chunk + by) * width, width), width)
        pairs.append((source.at[:, start : start + width], target.at[:, at]))
        start += width
    return pairs


def merge_kernel(
    result_a, result_b, got_a, gates_a, gates_got, gates_b, hidden_ref, gq_ref, gk_ref, gv_ref, gi_ref, gf_ref, sems
):
    chip, core = place()
    rows = got_a.shape[0]
    heads = gi_ref.shape[0]
    targets = (gq_ref, gk_ref, gv_ref, hidden_ref)
    mine = pl.ds(pl.multiple_of(core * rows, rows), rows)
    pairs = placed(result_a.at[mine, :], targets, 0, core)
    pairs += placed(result_b.at[mine, :], targets, 1, core)
    pairs += placed(got_a, targets, 0, 1 - core)
    copies = run_copies(pairs, sems)
    gates = jnp.where(chip == 0, gates_a[...] + gates_got[...], gates_b[...])
    gi_ref[...] = gates[:heads]
    gf_ref[...] = gates[heads:]
    for copy in copies:
        copy.wait()


def last_kernel(got_b, h_in, q_in, k_in, v_in, hidden_ref, gq_ref, gk_ref, gv_ref, sems):
    core = place()[1]
    for copy in run_copies(placed(got_b, (gq_ref, gk_ref, gv_ref, hidden_ref), 1, 1 - core), sems):
        copy.wait()


def split_shards(queries, keys, values, cotangent, igate, fgate, lengths):
    rows = queries.shape[0]
    heads = igate.shape[0]
    qk = queries.shape[1] // (4 * heads)
    vw = values.shape[1] // (4 * heads)
    width = heads * (qk + vw)
    bf16, f32 = jnp.bfloat16, jnp.float32
    shape = jax.ShapeDtypeStruct
    vmem = pl.BlockSpec(memory_space=pltpu.VMEM)
    smem = pl.BlockSpec(memory_space=pltpu.SMEM)
    hbm = pl.BlockSpec(memory_space=pltpu.HBM)
    params = pltpu.CompilerParams(vmem_limit_bytes=32 * 1024 * 1024)
    costly = pl.CostEstimate(flops=4 * 10**10, bytes_accessed=0, transcendentals=0)
    dma = pltpu.SemaphoreType.DMA

    def swap(value, mask):
        return lax.ppermute(value, "head", [(s, s ^ mask) for s in range(4)])

    cross_shape = shape((rows, width), bf16)
    own_shape = shape((2, rows, width), bf16)
    slots = igate.shape[1]
    to_core, a2, a3, own_qg, own_kv, gates = pl.pallas_call(
        pack_kernel,
        out_shape=(shape((rows, 4 * width), bf16), cross_shape, cross_shape, own_shape, own_shape)
        + (shape((2 * heads, slots), f32),),
        in_specs=[hbm] * 6,
        out_specs=(vmem,) * 6,
        scratch_shapes=[pltpu.VMEM(igate.shape, f32), pltpu.VMEM(igate.shape, f32), dma((22,))],
        compiler_params=params,
    )(*(pltpu.with_memory_space_constraint(a, pltpu.HBM) for a in (queries, keys, values, cotangent, igate, fgate)))
    from_core = swap(to_core, 1)
    gates_got = swap(gates, 2)
    a2, a3 = swap(a2, 2), swap(a3, 3)
    both = shape((2, 2 * rows, width), bf16)
    qg, kv, send, stats = pl.pallas_call(
        functools.partial(local_kernel, qk, vw),
        out_shape=(both, both, shape((2 * rows, width), bf16), shape((4 * heads, slots), f32)),
        in_specs=[smem] + [vmem] * 5,
        out_specs=(vmem,) * 4,
        cost_estimate=costly,
        compiler_params=params,
    )(lengths, own_qg, own_kv, from_core, gates, gates_got)
    stats = swap(stats, 2)
    chunk_b = swap(send, 2)

    def cross(chunk, *received):
        return pl.pallas_call(
            functools.partial(cross_kernel, chunk, qk, vw),
            out_shape=(shape((2 * rows, 2 * width), bf16), shape((rows, 2 * width), bf16), shape(gates.shape, f32)),
            in_specs=[smem] + [vmem] * (5 + len(received)),
            out_specs=(vmem,) * 3,
            cost_estimate=costly,
            scratch_shapes=[pltpu.VMEM((4 * rows, width), bf16)],
            compiler_params=params,
        )(lengths, qg, kv, gates, gates_got, stats, *received)

    result_a, theirs_a, gates_a = cross(0, a2, a3)
    gates_back = swap(gates_a, 2)
    got_a = swap(theirs_a, 1)
    result_b, theirs_b, gates_b = cross(1, chunk_b)
    theirs_b, gates_back = lax.optimization_barrier((theirs_b, gates_back))
    got_b = swap(theirs_b, 1)
    out_shape = tuple(shape(a.shape, bf16) for a in (values, queries, keys, values))
    gate_shape = shape(igate.shape, f32)
    *outputs, grad_in, grad_forget = pl.pallas_call(
        merge_kernel,
        out_shape=out_shape + (gate_shape, gate_shape),
        in_specs=[vmem] * 6,
        out_specs=(hbm,) * 4 + (vmem,) * 2,
        scratch_shapes=[dma((12,))],
        compiler_params=params,
    )(result_a, result_b, got_a, gates_a, gates_back, gates_b)
    outputs = pl.pallas_call(
        last_kernel,
        out_shape=out_shape,
        in_specs=[vmem] + [hbm] * 4,
        out_specs=(hbm,) * 4,
        scratch_shapes=[dma((4,))],
        input_output_aliases={1: 0, 2: 1, 3: 2, 4: 3},
        compiler_params=params,
    )(got_b, *outputs)
    return (*outputs, grad_in, grad_forget)


def shards(*arrays):
    if lax.axis_size("head") == 4:
        return split_shards(*arrays)
    return swapped_shards(*arrays)


def solution(mesh):
    rows = P(("groups", "seq", "head"), None)
    gates = P("head", ("groups", "seq"))
    return jax.shard_map(
        shards,
        mesh=mesh,
        in_specs=(rows, rows, rows, rows, gates, gates, P(("groups", "seq"))),
        out_specs=(rows, rows, rows, rows, gates, gates),
        check_vma=False,
    )
```

```python
import functools

import jax
import jax.numpy as jnp
from jax import lax
from jax.experimental import pallas as pl
from jax.experimental.pallas import tpu as pltpu
from jax.sharding import PartitionSpec as P

FAR = -1e30


def dot(left, right, contract):
    return lax.dot_general(left, right, (contract, ((), ())), preferred_element_type=jnp.float32)


def halves(value):
    high = value.astype(jnp.bfloat16)
    return high, (value - high.astype(jnp.float32)).astype(jnp.bfloat16)


def wide_dot(left, right, contract):
    rows = left.shape[0]
    both = dot(jnp.concatenate(halves(left), axis=0), right, contract)
    return both[:rows] + both[rows:]


NN = ((1,), (0,))
NT = ((1,), (1,))
TN = ((0,), (0,))


def log_sigmoid(value):
    return jnp.minimum(value, 0.0) - jnp.log(1.0 + jnp.exp(-jnp.abs(value)))


def decay(in_gate, forget_gate, length, scale):
    size = in_gate.shape[1]
    rows = lax.broadcasted_iota(jnp.int32, (size, size), 0)
    cols = lax.broadcasted_iota(jnp.int32, (size, size), 1)
    logs = jnp.where(cols[:1] < length, log_sigmoid(forget_gate), 0.0)
    total_col = jnp.sum(jnp.where(cols <= rows, logs, 0.0), axis=1, keepdims=True)
    total_row = jnp.sum(jnp.where(cols == rows, total_col, 0.0), axis=0, keepdims=True)
    mask = (cols <= rows) & (rows < length)
    return jnp.exp(jnp.where(mask, total_col - total_row, FAR)) * (jnp.exp(in_gate) * scale)


def whole_kernel(heads, qk, vw, length_ref, x_ref, ig_ref, fg_ref, out_ref, gi_ref, gf_ref):
    length = length_ref[0]
    size = x_ref.shape[0]
    rows = lax.broadcasted_iota(jnp.int32, (size, size), 0)
    cols = lax.broadcasted_iota(jnp.int32, (size, size), 1)
    for head in range(heads):
        q = x_ref[:, head * qk : (head + 1) * qk]
        k = x_ref[:, (heads + head) * qk : (heads + head + 1) * qk]
        v0 = 2 * heads * qk + head * vw
        g0 = v0 + heads * vw
        v = x_ref[:, v0 : v0 + vw]
        g = x_ref[:, g0 : g0 + vw]
        forget = fg_ref[head : head + 1, :]
        weight = decay(ig_ref[head : head + 1, :], forget, length, qk**-0.5)
        scores = dot(q, k, NT) * weight
        pulled = dot(g, v, NT)
        norm = jnp.sum(scores, axis=1, keepdims=True)
        along = jnp.sum(scores * pulled, axis=1, keepdims=True)
        size_of = jnp.abs(norm)
        inverse = 1.0 / jnp.maximum(size_of, 1.0)
        share = jnp.where(size_of > 1.0, 1.0, jnp.where(size_of == 1.0, 0.5, 0.0))
        grad_norm = -along * inverse * inverse * share * jnp.where(norm < 0.0, -1.0, 1.0)
        grad_scores = pulled * inverse + grad_norm
        hidden = wide_dot(scores * inverse, v, NN)
        grad_raw = grad_scores * weight
        gq = wide_dot(grad_raw, k, NN)
        gk = wide_dot(grad_raw.T, q, NN)
        gv = wide_dot((scores * inverse).T, g, NN)
        out_ref[:, head * qk : (head + 1) * qk] = gq.astype(jnp.bfloat16)
        out_ref[:, (heads + head) * qk : (heads + head + 1) * qk] = gk.astype(jnp.bfloat16)
        out_ref[:, v0 : v0 + vw] = gv.astype(jnp.bfloat16)
        out_ref[:, g0 : g0 + vw] = hidden.astype(jnp.bfloat16)
        by_column = jnp.sum(grad_scores * scores, axis=0, keepdims=True)
        by_row = along * inverse * (1.0 - share)
        moved = by_row - jnp.sum(jnp.where(rows == cols, by_column, 0.0), axis=1, keepdims=True)
        grad_log = jnp.sum(jnp.where(rows >= cols, moved, 0.0), axis=0, keepdims=True)
        gi_ref[head : head + 1, :] = by_column
        gf_ref[head : head + 1, :] = jnp.where(
            cols[:1] < length, grad_log / (1.0 + jnp.exp(forget)), 0.0
        )


def swapped_shards(queries, keys, values, cotangent, igate, fgate, lengths):
    devices = lax.axis_size("head")
    rows = queries.shape[0]
    heads = igate.shape[0]
    qk = queries.shape[1] // (devices * heads)
    vw = values.shape[1] // (devices * heads)
    parts = [a.reshape(rows, devices, -1) for a in (queries, keys, values, cotangent)]
    joined = jnp.concatenate(parts, axis=2)
    here = lax.all_to_all(joined, "head", split_axis=1, concat_axis=0, tiled=True)
    here = here.reshape(rows * devices, -1)
    vmem = pl.BlockSpec(memory_space=pltpu.VMEM)
    out, grad_in, grad_forget = pl.pallas_call(
        functools.partial(whole_kernel, heads, qk, vw),
        out_shape=(
            jax.ShapeDtypeStruct(here.shape, jnp.bfloat16),
            jax.ShapeDtypeStruct(igate.shape, jnp.float32),
            jax.ShapeDtypeStruct(igate.shape, jnp.float32),
        ),
        in_specs=[pl.BlockSpec(memory_space=pltpu.SMEM), vmem, vmem, vmem],
        out_specs=(vmem, vmem, vmem),
        compiler_params=pltpu.CompilerParams(vmem_limit_bytes=32 * 1024 * 1024),
    )(lengths, here, igate, fgate)
    back = lax.all_to_all(
        out.reshape(devices, rows, -1), "head", split_axis=0, concat_axis=0, tiled=True
    )
    back = back.transpose(1, 0, 2)
    ends = [0, heads * qk, 2 * heads * qk, 2 * heads * qk + heads * vw, back.shape[2]]
    gq, gk, gv, hidden = [
        back[:, :, a:b].reshape(rows, -1) for a, b in zip(ends[:-1], ends[1:])
    ]
    return hidden, gq, gk, gv, grad_in, grad_forget


def backward_terms(norm, along):
    size = jnp.abs(norm)
    inverse = 1.0 / jnp.maximum(size, 1.0)
    share = jnp.where(size > 1.0, 1.0, jnp.where(size == 1.0, 0.5, 0.0))
    grad_norm = -along * inverse * inverse * share * jnp.where(norm < 0.0, -1.0, 1.0)
    return inverse, grad_norm, along * inverse * (1.0 - share)


def place():
    me = lax.axis_index("head")
    return me // 2, lax.rem(me, 2)


def run_copies(pairs, sems):
    copies = [pltpu.make_async_copy(a, b, sems.at[i]) for i, (a, b) in enumerate(pairs)]
    for copy in copies:
        copy.start()
    return copies


def block(ref, owner):
    width = ref.shape[1] // 4
    return ref.at[:, pl.ds(pl.multiple_of(owner * width, width), width)]


def block_copies(refs, owner, target):
    split = refs[0].shape[1] // 4
    end = split + refs[1].shape[1] // 4
    return [(block(refs[0], owner), target.at[:, :split]), (block(refs[1], owner), target.at[:, split:end])]


def copy_for_chip(moves, inputs, sems):
    q_ref, k_ref, v_ref, g_ref = inputs
    chip = place()[0]

    @pl.when(chip == 0)
    def _():
        run_copies(moves((k_ref, v_ref), (q_ref, g_ref)), sems)

    @pl.when(chip != 0)
    def _():
        run_copies(moves((q_ref, g_ref), (k_ref, v_ref)), sems)

    pairs = moves((k_ref, v_ref), (q_ref, g_ref))
    return [pltpu.make_async_copy(source, target, sems.at[i]) for i, (source, target) in enumerate(pairs)]


def pack_kernel(
    q_ref, k_ref, v_ref, g_ref, ig_ref, fg_ref, a2_ref, a3_ref, b2_ref, b3_ref, rest_ref, m1_ref, gates_ref,
    in_ref, out_ref, sems,
):
    core = place()[1]
    heads = ig_ref.shape[0]
    width = b2_ref.shape[1]

    def moves(sent, kept):
        pairs = [(ig_ref, in_ref), (fg_ref, out_ref)]
        for chunk, (same, other) in enumerate(((a2_ref, a3_ref), (b2_ref, b3_ref))):
            pairs += block_copies(sent, 2 * chunk + core, same) + block_copies(sent, 2 * chunk + 1 - core, other)
            pairs += block_copies(kept, 2 * chunk + core, rest_ref.at[chunk])
            for i, refs in enumerate((sent, kept)):
                start = (2 * chunk + i) * width
                pairs += block_copies(refs, 2 * chunk + 1 - core, m1_ref.at[:, start : start + width])
        return pairs

    copies = copy_for_chip(moves, (q_ref, k_ref, v_ref, g_ref), sems)
    for copy in copies[:2]:
        copy.wait()
    gates_ref[:heads, :] = in_ref[...]
    gates_ref[heads:, :] = out_ref[...]
    for copy in copies[2:]:
        copy.wait()


def local_kernel(
    qk, vw, length_ref, a2_ref, b2_ref, rest_ref, m1_ref, own_ref, got_ref, qg_ref, kv_ref, stats_ref
):
    chip, core = place()
    rows = m1_ref.shape[0]
    heads = own_ref.shape[0] // 2
    wq, wv = heads * qk, heads * vw
    width = wq + wv
    mine = pl.ds(pl.multiple_of(core * rows, rows), rows)
    theirs = pl.ds(pl.multiple_of((1 - core) * rows, rows), rows)

    def gather(sent, kept):
        for chunk, own in enumerate((a2_ref, b2_ref)):
            start = chunk * 2 * width
            sent[chunk, mine, :] = own[...]
            sent[chunk, theirs, :] = m1_ref[:, start : start + width]
            kept[chunk, mine, :] = rest_ref[chunk]
            kept[chunk, theirs, :] = m1_ref[:, start + width : start + 2 * width]

    stats_ref[...] = jnp.zeros_like(stats_ref)
    length = length_ref[0]

    def part(side, chunk):
        gates = own_ref if side == chunk else got_ref
        size = 2 * rows
        low = side * size
        for head in range(heads):
            q = qg_ref[chunk, :, head * qk : (head + 1) * qk]
            k = kv_ref[chunk, :, head * qk : (head + 1) * qk]
            g = qg_ref[chunk, :, wq + head * vw : wq + (head + 1) * vw]
            v = kv_ref[chunk, :, wq + head * vw : wq + (head + 1) * vw]
            weight = decay(gates[head : head + 1, :], gates[heads + head : heads + head + 1, :], length, qk**-0.5)
            weight = weight[low : low + size, low : low + size]
            scores = dot(q, k, NT) * weight
            pulled = dot(g, v, NT)
            norm = jnp.sum(scores, axis=1, keepdims=True)
            along = jnp.sum(scores * pulled, axis=1, keepdims=True)
            on = lax.broadcasted_iota(jnp.int32, (size, 2 * size), 0) + low == lax.broadcasted_iota(
                jnp.int32, (size, 2 * size), 1
            )

            def as_row(column):
                return jnp.sum(jnp.where(on, column, 0.0), axis=0, keepdims=True)

            if side == 1:
                at = chunk * heads + head
                stats_ref[at : at + 1, :] = as_row(norm)
                stats_ref[2 * heads + at : 2 * heads + at + 1, :] = as_row(along)
            else:
                inverse, grad_norm, by_row = backward_terms(norm, along)
                by_column = jnp.sum((pulled * inverse + grad_norm) * scores, axis=0, keepdims=True)
                stats_ref[head : head + 1, :size] = by_column
                stats_ref[heads + head : heads + head + 1, :] = as_row(by_row)

    @pl.when(chip == 0)
    def _():
        gather(kv_ref, qg_ref)
        part(0, 1)

    @pl.when(chip != 0)
    def _():
        gather(qg_ref, kv_ref)
        part(1, 0)
        part(1, 1)


def placed(source, targets, chunk, by):
    pairs = []
    start = 0
    for target in targets:
        width = target.shape[1] // 4
        at = pl.ds(pl.multiple_of((2 * chunk + by) * width, width), width)
        pairs.append((source.at[:, start : start + width], target.at[:, at]))
        start += width
    return pairs


def cross_kernel(
    chunk, qk, vw, length_ref, qg_ref, kv_ref, own_ref, got_ref, stats_ref, same_ref, other_ref, *refs
):
    chip, core = place()
    writes = []
    if chunk == 0:
        result_ref, theirs_ref, gates_ref, wide_ref = refs
    else:
        result_a, result_ref, theirs_ref, gates_ref, *outputs, wide_ref, sems = refs
        rows = theirs_ref.shape[0]
        mine_a = result_a.at[pl.ds(pl.multiple_of(core * rows, rows), rows), :]
        writes = run_copies(placed(mine_a, outputs, 0, core), sems)
    rows = theirs_ref.shape[0]
    size = 2 * rows
    heads = own_ref.shape[0] // 2
    wq, wv = heads * qk, heads * vw

    def gather(side, local):
        base = 0 if side else size
        wide_ref[side * size : (side + 1) * size, :] = local[chunk]
        for ref, by in ((same_ref, core), (other_ref, 1 - core)):
            wide_ref[pl.ds(pl.multiple_of(base + by * rows, rows), rows), :] = ref[...]

    length = length_ref[0]
    gates_ref[...] = jnp.zeros_like(gates_ref)

    def part(side):
        gather(side, kv_ref if side else qg_ref)
        thin = (qg_ref if side else kv_ref).at[chunk]
        gates = own_ref if side == chunk else got_ref
        full = 2 * size
        rows_at = lax.broadcasted_iota(jnp.int32, (full, full), 0)
        cols_at = lax.broadcasted_iota(jnp.int32, (full, full), 1)

        def as_column(row):
            return jnp.sum(jnp.where(rows_at == cols_at, row, 0.0), axis=1, keepdims=True)

        weights = [
            decay(gates[head : head + 1, :], gates[heads + head : heads + head + 1, :], length, qk**-0.5)
            for head in range(heads)
        ]
        for head in range(heads):
            first = slice(head * qk, (head + 1) * qk)
            second = slice(wq + head * vw, wq + (head + 1) * vw)
            if side == 0:
                q, g, k, v = wide_ref[:, first], wide_ref[:, second], thin[:, first], thin[:, second]
                weight = weights[head][:, :size]
            else:
                k, v, q, g = wide_ref[:, first], wide_ref[:, second], thin[:, first], thin[:, second]
                weight = weights[head][size:, :]
            scores = dot(q, k, NT) * weight
            pulled = dot(g, v, NT)
            norm = jnp.sum(scores, axis=1, keepdims=True)
            along = jnp.sum(scores * pulled, axis=1, keepdims=True)
            if side == 0:
                at = chunk * heads + head
                norm = norm + as_column(stats_ref[at : at + 1, :])
                along = along + as_column(stats_ref[2 * heads + at : 2 * heads + at + 1, :])
            inverse, grad_norm, by_row = backward_terms(norm, along)
            grad_scores = pulled * inverse + grad_norm
            scaled = scores * inverse
            grad_raw = grad_scores * weight
            if side == 0:
                hidden = wide_dot(scaled[:size], v, NN)
                gq = wide_dot(grad_raw[:size], k, NN)
                gk = wide_dot(grad_raw.T, q, NN)
                gv = wide_dot(scaled.T, g, NN)
            else:
                hidden = wide_dot(scaled, v, NN)
                gq = wide_dot(grad_raw, k, NN)
                gk = wide_dot(grad_raw.T[size:], q, NN)
                gv = wide_dot(scaled.T[size:], g, NN)
            result_ref[:, head * qk : (head + 1) * qk] = gq.astype(jnp.bfloat16)
            result_ref[:, wq + head * qk : wq + (head + 1) * qk] = gk.astype(jnp.bfloat16)
            result_ref[:, 2 * wq + head * vw : 2 * wq + (head + 1) * vw] = gv.astype(jnp.bfloat16)
            result_ref[:, 2 * wq + wv + head * vw : 2 * wq + wv + (head + 1) * vw] = hidden.astype(jnp.bfloat16)
            by_column = jnp.sum(grad_scores * scores, axis=0, keepdims=True)
            forget = gates[heads + head : heads + head + 1, :]
            live = cols_at[:1] < length
            slope = jnp.where(live, 1.0 / (1.0 + jnp.exp(forget)), 0.0)
            if side == 0 and chunk == 0:
                small_rows, small_cols = rows_at[:size, :size], cols_at[:size, :size]
                column = jnp.sum(jnp.where(small_rows == small_cols, by_column, 0.0), axis=1, keepdims=True)
                before = jnp.where(small_rows < small_cols, column - by_row[:size], 0.0)
                grad_log = jnp.sum(before, axis=0, keepdims=True)
                gates_ref[head : head + 1, :size] = by_column
                gates_ref[heads + head : heads + head + 1, :size] = grad_log * slope[:, :size]
            if side == 1:
                row = jnp.sum(jnp.where(rows_at[size:] == cols_at[size:], by_row, 0.0), axis=0, keepdims=True)
                if chunk == 1:
                    by_column = by_column + stats_ref[head : head + 1, :]
                    row = row + stats_ref[heads + head : heads + head + 1, :]
                    seen = jnp.full((1, full), True)
                else:
                    seen = cols_at[:1] >= size
                by_column = jnp.where(seen, by_column, 0.0)
                moved = as_column(row - by_column)
                grad_log = jnp.sum(jnp.where(rows_at >= cols_at, moved, 0.0), axis=0, keepdims=True)
                gates_ref[head : head + 1, :] = by_column
                gates_ref[heads + head : heads + head + 1, :] = jnp.where(seen, grad_log * slope, 0.0)
        theirs_ref[...] = result_ref[pl.ds(pl.multiple_of((1 - core) * rows, rows), rows), :]

    @pl.when(chip == 0)
    def _():
        part(0)

    @pl.when(chip != 0)
    def _():
        part(1)

    for copy in writes:
        copy.wait()


def merge_kernel(result_b, got_a, gates_a, gates_got, gates_b, *refs):
    *outputs, gi_ref, gf_ref, gates_ref, sems = refs[4:]
    chip, core = place()
    rows = got_a.shape[0]
    heads = gi_ref.shape[0]
    mine = result_b.at[pl.ds(pl.multiple_of(core * rows, rows), rows), :]
    copies = run_copies(placed(mine, outputs, 1, core) + placed(got_a, outputs, 0, 1 - core), sems)
    gates = jnp.where(chip == 0, gates_a[...] + gates_got[...], gates_b[...])
    gates_ref[0] = gates[:heads]
    gates_ref[1] = gates[heads:]
    copies += run_copies([(gates_ref.at[0], gi_ref), (gates_ref.at[1], gf_ref)], sems.at[pl.ds(8, 2)])
    for copy in copies:
        copy.wait()


def last_kernel(got_b, *refs):
    *outputs, sems = refs[4:]
    for copy in run_copies(placed(got_b, outputs, 1, 1 - place()[1]), sems):
        copy.wait()


def split_shards(queries, keys, values, cotangent, igate, fgate, lengths):
    rows = queries.shape[0]
    heads = igate.shape[0]
    qk = queries.shape[1] // (4 * heads)
    vw = values.shape[1] // (4 * heads)
    width = heads * (qk + vw)
    bf16, f32 = jnp.bfloat16, jnp.float32
    shape = jax.ShapeDtypeStruct
    vmem = pl.BlockSpec(memory_space=pltpu.VMEM)
    smem = pl.BlockSpec(memory_space=pltpu.SMEM)
    hbm = pl.BlockSpec(memory_space=pltpu.HBM)
    params = pltpu.CompilerParams(vmem_limit_bytes=32 * 1024 * 1024)
    costly = pl.CostEstimate(flops=4 * 10**10, bytes_accessed=0, transcendentals=0)
    dma = pltpu.SemaphoreType.DMA

    def swap(value, mask):
        return lax.ppermute(value, "head", [(s, s ^ mask) for s in range(4)])

    slots = igate.shape[1]
    gates_shape = shape((2 * heads, slots), f32)
    arrays = [pltpu.with_memory_space_constraint(a, pltpu.HBM) for a in (queries, keys, values, cotangent, igate, fgate)]
    cross_shape = shape((rows, width), bf16)
    a2_sent, a3, b2_sent, b3, rest, to_core, gates = pl.pallas_call(
        pack_kernel,
        out_shape=(cross_shape,) * 4 + (shape((2, rows, width), bf16), shape((rows, 4 * width), bf16), gates_shape),
        in_specs=[hbm] * 6,
        out_specs=(vmem,) * 7,
        scratch_shapes=[pltpu.VMEM(igate.shape, f32), pltpu.VMEM(igate.shape, f32), dma((22,))],
        compiler_params=params,
    )(*arrays)
    from_core = swap(to_core, 1)
    gates_got = swap(gates, 2)
    a2, a3 = swap(a2_sent, 2), swap(a3, 3)
    both = shape((2, 2 * rows, width), bf16)
    qg, kv, stats = pl.pallas_call(
        functools.partial(local_kernel, qk, vw),
        out_shape=(both, both, shape((4 * heads, slots), f32)),
        in_specs=[smem] + [vmem] * 6,
        out_specs=(vmem,) * 3,
        cost_estimate=costly,
        compiler_params=params,
    )(lengths, a2_sent, b2_sent, rest, from_core, gates, gates_got)
    stats = swap(stats, 2)
    b2, b3 = swap(b2_sent, 2), swap(b3, 3)
    out_shape = tuple(shape(a.shape, bf16) for a in (queries, keys, values, values))

    def cross(chunk, received, written):
        return pl.pallas_call(
            functools.partial(cross_kernel, chunk, qk, vw),
            out_shape=(shape((2 * rows, 2 * width), bf16), shape((rows, 2 * width), bf16), gates_shape)
            + (out_shape if written else ()),
            in_specs=[smem] + [vmem] * (7 + len(written)),
            out_specs=(vmem,) * 3 + ((hbm,) * 4 if written else ()),
            scratch_shapes=[pltpu.VMEM((4 * rows, width), bf16)] + ([dma((4,))] if written else []),
            cost_estimate=costly,
            compiler_params=params,
        )(lengths, qg, kv, gates, gates_got, stats, *received, *written)

    result_a, theirs_a, gates_a = cross(0, (a2, a3), ())
    gates_back = swap(gates_a, 2)
    got_a = swap(theirs_a, 1)
    result_b, theirs_b, gates_b, *outputs = cross(1, (b2, b3), (result_a,))
    got_b = swap(theirs_b, 1)
    gate_shape = shape(igate.shape, f32)
    *outputs, grad_in, grad_forget = pl.pallas_call(
        merge_kernel,
        out_shape=out_shape + (gate_shape, gate_shape),
        in_specs=[vmem] * 5 + [hbm] * 4,
        out_specs=(hbm,) * 6,
        scratch_shapes=[pltpu.VMEM((2, *igate.shape), f32), dma((10,))],
        cost_estimate=costly,
        input_output_aliases={5: 0, 6: 1, 7: 2, 8: 3},
        compiler_params=params,
    )(result_b, got_a, gates_a, gates_back, gates_b, *outputs)
    gq, gk, gv, hidden = pl.pallas_call(
        last_kernel,
        out_shape=out_shape,
        in_specs=[vmem] + [hbm] * 4,
        out_specs=(hbm,) * 4,
        scratch_shapes=[dma((4,))],
        input_output_aliases={1: 0, 2: 1, 3: 2, 4: 3},
        compiler_params=params,
    )(got_b, *outputs)
    return hidden, gq, gk, gv, grad_in, grad_forget


def shards(*arrays):
    if lax.axis_size("head") == 4:
        return split_shards(*arrays)
    return swapped_shards(*arrays)


def solution(mesh):
    rows = P(("groups", "seq", "head"), None)
    gates = P("head", ("groups", "seq"))
    return jax.shard_map(
        shards,
        mesh=mesh,
        in_specs=(rows, rows, rows, rows, gates, gates, P(("groups", "seq"))),
        out_specs=(rows, rows, rows, rows, gates, gates),
        check_vma=False,
    )
```

```python
import functools

import jax
import jax.numpy as jnp
from jax import lax
from jax.experimental import pallas as pl
from jax.experimental.pallas import tpu as pltpu
from jax.sharding import PartitionSpec as P

FAR = -1e30


def dot(left, right, contract):
    return lax.dot_general(left, right, (contract, ((), ())), preferred_element_type=jnp.float32)


def halves(value):
    high = value.astype(jnp.bfloat16)
    return high, (value - high.astype(jnp.float32)).astype(jnp.bfloat16)


def wide_dot(left, right, contract):
    rows = left.shape[0]
    both = dot(jnp.concatenate(halves(left), axis=0), right, contract)
    return both[:rows] + both[rows:]


NN = ((1,), (0,))
NT = ((1,), (1,))
TN = ((0,), (0,))


def log_sigmoid(value):
    return jnp.minimum(value, 0.0) - jnp.log(1.0 + jnp.exp(-jnp.abs(value)))


def decay(in_gate, forget_gate, length, scale):
    size = in_gate.shape[1]
    rows = lax.broadcasted_iota(jnp.int32, (size, size), 0)
    cols = lax.broadcasted_iota(jnp.int32, (size, size), 1)
    logs = jnp.where(cols[:1] < length, log_sigmoid(forget_gate), 0.0)
    total_col = jnp.sum(jnp.where(cols <= rows, logs, 0.0), axis=1, keepdims=True)
    total_row = jnp.sum(jnp.where(cols == rows, total_col, 0.0), axis=0, keepdims=True)
    mask = (cols <= rows) & (rows < length)
    return jnp.exp(jnp.where(mask, total_col - total_row, FAR)) * (jnp.exp(in_gate) * scale)


def whole_kernel(heads, qk, vw, length_ref, x_ref, ig_ref, fg_ref, out_ref, gi_ref, gf_ref):
    length = length_ref[0]
    size = x_ref.shape[0]
    rows = lax.broadcasted_iota(jnp.int32, (size, size), 0)
    cols = lax.broadcasted_iota(jnp.int32, (size, size), 1)
    for head in range(heads):
        q = x_ref[:, head * qk : (head + 1) * qk]
        k = x_ref[:, (heads + head) * qk : (heads + head + 1) * qk]
        v0 = 2 * heads * qk + head * vw
        g0 = v0 + heads * vw
        v = x_ref[:, v0 : v0 + vw]
        g = x_ref[:, g0 : g0 + vw]
        forget = fg_ref[head : head + 1, :]
        weight = decay(ig_ref[head : head + 1, :], forget, length, qk**-0.5)
        scores = dot(q, k, NT) * weight
        pulled = dot(g, v, NT)
        norm = jnp.sum(scores, axis=1, keepdims=True)
        along = jnp.sum(scores * pulled, axis=1, keepdims=True)
        size_of = jnp.abs(norm)
        inverse = 1.0 / jnp.maximum(size_of, 1.0)
        share = jnp.where(size_of > 1.0, 1.0, jnp.where(size_of == 1.0, 0.5, 0.0))
        grad_norm = -along * inverse * inverse * share * jnp.where(norm < 0.0, -1.0, 1.0)
        grad_scores = pulled * inverse + grad_norm
        hidden = wide_dot(scores * inverse, v, NN)
        grad_raw = grad_scores * weight
        gq = wide_dot(grad_raw, k, NN)
        gk = wide_dot(grad_raw.T, q, NN)
        gv = wide_dot((scores * inverse).T, g, NN)
        out_ref[:, head * qk : (head + 1) * qk] = gq.astype(jnp.bfloat16)
        out_ref[:, (heads + head) * qk : (heads + head + 1) * qk] = gk.astype(jnp.bfloat16)
        out_ref[:, v0 : v0 + vw] = gv.astype(jnp.bfloat16)
        out_ref[:, g0 : g0 + vw] = hidden.astype(jnp.bfloat16)
        by_column = jnp.sum(grad_scores * scores, axis=0, keepdims=True)
        by_row = along * inverse * (1.0 - share)
        moved = by_row - jnp.sum(jnp.where(rows == cols, by_column, 0.0), axis=1, keepdims=True)
        grad_log = jnp.sum(jnp.where(rows >= cols, moved, 0.0), axis=0, keepdims=True)
        gi_ref[head : head + 1, :] = by_column
        gf_ref[head : head + 1, :] = jnp.where(
            cols[:1] < length, grad_log / (1.0 + jnp.exp(forget)), 0.0
        )


def swapped_shards(queries, keys, values, cotangent, igate, fgate, lengths):
    devices = lax.axis_size("head")
    rows = queries.shape[0]
    heads = igate.shape[0]
    qk = queries.shape[1] // (devices * heads)
    vw = values.shape[1] // (devices * heads)
    parts = [a.reshape(rows, devices, -1) for a in (queries, keys, values, cotangent)]
    joined = jnp.concatenate(parts, axis=2)
    here = lax.all_to_all(joined, "head", split_axis=1, concat_axis=0, tiled=True)
    here = here.reshape(rows * devices, -1)
    vmem = pl.BlockSpec(memory_space=pltpu.VMEM)
    out, grad_in, grad_forget = pl.pallas_call(
        functools.partial(whole_kernel, heads, qk, vw),
        out_shape=(
            jax.ShapeDtypeStruct(here.shape, jnp.bfloat16),
            jax.ShapeDtypeStruct(igate.shape, jnp.float32),
            jax.ShapeDtypeStruct(igate.shape, jnp.float32),
        ),
        in_specs=[pl.BlockSpec(memory_space=pltpu.SMEM), vmem, vmem, vmem],
        out_specs=(vmem, vmem, vmem),
        compiler_params=pltpu.CompilerParams(vmem_limit_bytes=32 * 1024 * 1024),
    )(lengths, here, igate, fgate)
    back = lax.all_to_all(
        out.reshape(devices, rows, -1), "head", split_axis=0, concat_axis=0, tiled=True
    )
    back = back.transpose(1, 0, 2)
    ends = [0, heads * qk, 2 * heads * qk, 2 * heads * qk + heads * vw, back.shape[2]]
    gq, gk, gv, hidden = [
        back[:, :, a:b].reshape(rows, -1) for a, b in zip(ends[:-1], ends[1:])
    ]
    return hidden, gq, gk, gv, grad_in, grad_forget


def backward_terms(norm, along):
    size = jnp.abs(norm)
    inverse = 1.0 / jnp.maximum(size, 1.0)
    share = jnp.where(size > 1.0, 1.0, jnp.where(size == 1.0, 0.5, 0.0))
    grad_norm = -along * inverse * inverse * share * jnp.where(norm < 0.0, -1.0, 1.0)
    return inverse, grad_norm, along * inverse * (1.0 - share)


def place():
    me = lax.axis_index("head")
    return me // 2, lax.rem(me, 2)


def run_copies(pairs, sems):
    copies = [pltpu.make_async_copy(a, b, sems.at[i]) for i, (a, b) in enumerate(pairs)]
    for copy in copies:
        copy.start()
    return copies


def block(ref, owner):
    width = ref.shape[1] // 4
    return ref.at[:, pl.ds(pl.multiple_of(owner * width, width), width)]


def block_copies(refs, owner, target):
    split = refs[0].shape[1] // 4
    end = split + refs[1].shape[1] // 4
    return [(block(refs[0], owner), target.at[:, :split]), (block(refs[1], owner), target.at[:, split:end])]


def copy_for_chip(moves, inputs, sems):
    q_ref, k_ref, v_ref, g_ref = inputs
    chip = place()[0]

    @pl.when(chip == 0)
    def _():
        run_copies(moves((k_ref, v_ref), (q_ref, g_ref)), sems)

    @pl.when(chip != 0)
    def _():
        run_copies(moves((q_ref, g_ref), (k_ref, v_ref)), sems)

    pairs = moves((k_ref, v_ref), (q_ref, g_ref))
    return [pltpu.make_async_copy(source, target, sems.at[i]) for i, (source, target) in enumerate(pairs)]


def pack_kernel(
    q_ref, k_ref, v_ref, g_ref, ig_ref, fg_ref, a2_ref, d_ref, m1_ref, gates_ref, in_ref, out_ref, sems
):
    core = place()[1]
    heads = ig_ref.shape[0]
    width = a2_ref.shape[1]

    def moves(sent, kept):
        pairs = [(ig_ref, in_ref), (fg_ref, out_ref)]
        pairs += block_copies(sent, core, a2_ref)
        for chunk in range(2):
            pairs += block_copies(sent, 2 * chunk + 1 - core, d_ref.at[:, chunk * width : (chunk + 1) * width])
            for i, refs in enumerate((sent, kept)):
                start = (2 * chunk + i) * width
                pairs += block_copies(refs, 2 * chunk + 1 - core, m1_ref.at[:, start : start + width])
        return pairs

    copies = copy_for_chip(moves, (q_ref, k_ref, v_ref, g_ref), sems)
    for copy in copies[:2]:
        copy.wait()
    gates_ref[:heads, :] = in_ref[...]
    gates_ref[heads:, :] = out_ref[...]
    for copy in copies[2:]:
        copy.wait()


def rest_kernel(q_ref, k_ref, v_ref, g_ref, b2_ref, rest_ref, sems):
    core = place()[1]

    def moves(sent, kept):
        pairs = block_copies(sent, 2 + core, b2_ref)
        return pairs + block_copies(kept, core, rest_ref.at[0]) + block_copies(kept, 2 + core, rest_ref.at[1])

    for copy in copy_for_chip(moves, (q_ref, k_ref, v_ref, g_ref), sems):
        copy.wait()


def local_kernel(
    qk, vw, length_ref, a2_ref, b2_ref, rest_ref, m1_ref, own_ref, got_ref, qg_ref, kv_ref, stats_ref
):
    chip, core = place()
    rows = m1_ref.shape[0]
    heads = own_ref.shape[0] // 2
    wq, wv = heads * qk, heads * vw
    width = wq + wv
    mine = pl.ds(pl.multiple_of(core * rows, rows), rows)
    theirs = pl.ds(pl.multiple_of((1 - core) * rows, rows), rows)

    def gather(sent, kept):
        for chunk, own in enumerate((a2_ref, b2_ref)):
            start = chunk * 2 * width
            sent[chunk, mine, :] = own[...]
            sent[chunk, theirs, :] = m1_ref[:, start : start + width]
            kept[chunk, mine, :] = rest_ref[chunk]
            kept[chunk, theirs, :] = m1_ref[:, start + width : start + 2 * width]

    stats_ref[...] = jnp.zeros_like(stats_ref)
    length = length_ref[0]

    def part(side, chunks):
        size = 2 * rows
        low = side * size
        items = [(chunk, head) for chunk in chunks for head in range(heads)]
        scores, pulled = [], []
        for chunk, head in items:
            first = slice(head * qk, (head + 1) * qk)
            second = slice(wq + head * vw, wq + (head + 1) * vw)
            scores.append(dot(qg_ref[chunk, :, first], kv_ref[chunk, :, first], NT))
            pulled.append(dot(qg_ref[chunk, :, second], kv_ref[chunk, :, second], NT))
        for i, (chunk, head) in enumerate(items):
            gates = own_ref if side == chunk else got_ref
            weight = decay(gates[head : head + 1, :], gates[heads + head : heads + head + 1, :], length, qk**-0.5)
            scores[i] = scores[i] * weight[low : low + size, low : low + size]
        norms = [jnp.sum(score, axis=1, keepdims=True) for score in scores]
        alongs = [jnp.sum(score * pull, axis=1, keepdims=True) for score, pull in zip(scores, pulled)]
        on = lax.broadcasted_iota(jnp.int32, (size, 2 * size), 0) + low == lax.broadcasted_iota(
            jnp.int32, (size, 2 * size), 1
        )

        def as_row(column):
            return jnp.sum(jnp.where(on, column, 0.0), axis=0, keepdims=True)

        for (chunk, head), score, pull, norm, along in zip(items, scores, pulled, norms, alongs):
            if side == 1:
                at = chunk * heads + head
                stats_ref[at : at + 1, :] = as_row(norm)
                stats_ref[2 * heads + at : 2 * heads + at + 1, :] = as_row(along)
            else:
                inverse, grad_norm, by_row = backward_terms(norm, along)
                by_column = jnp.sum((pull * inverse + grad_norm) * score, axis=0, keepdims=True)
                stats_ref[head : head + 1, :size] = by_column
                stats_ref[heads + head : heads + head + 1, :] = as_row(by_row)

    @pl.when(chip == 0)
    def _():
        gather(kv_ref, qg_ref)
        part(0, (1,))

    @pl.when(chip != 0)
    def _():
        gather(qg_ref, kv_ref)
        part(1, (0, 1))


def placed(source, targets, chunk, by):
    pairs = []
    start = 0
    for target in targets:
        width = target.shape[1] // 4
        at = pl.ds(pl.multiple_of((2 * chunk + by) * width, width), width)
        pairs.append((source.at[:, start : start + width], target.at[:, at]))
        start += width
    return pairs


def cross_kernel(
    chunk, qk, vw, length_ref, qg_ref, kv_ref, own_ref, got_ref, stats_ref, same_ref, other_ref, *refs
):
    chip, core = place()
    writes = []
    if chunk == 0:
        result_ref, theirs_ref, gates_ref, wide_ref = refs
    else:
        result_a, result_ref, theirs_ref, gates_ref, *outputs, wide_ref, sems = refs
        rows = theirs_ref.shape[0]
        mine_a = result_a.at[pl.ds(pl.multiple_of(core * rows, rows), rows), :]
        writes = run_copies(placed(mine_a, outputs, 0, core), sems)
    rows = theirs_ref.shape[0]
    size = 2 * rows
    heads = own_ref.shape[0] // 2
    wq, wv = heads * qk, heads * vw

    def gather(side, local):
        base = 0 if side else size
        wide_ref[side * size : (side + 1) * size, :] = local[chunk]
        for ref, by in ((same_ref, core), (other_ref, 1 - core)):
            start = chunk * (wq + wv) if ref is other_ref else 0
            wide_ref[pl.ds(pl.multiple_of(base + by * rows, rows), rows), :] = ref[:, start : start + wq + wv]

    length = length_ref[0]
    gates_ref[...] = jnp.zeros_like(gates_ref)

    def part(side):
        gather(side, kv_ref if side else qg_ref)
        thin = (qg_ref if side else kv_ref).at[chunk]
        gates = own_ref if side == chunk else got_ref
        full = 2 * size
        rows_at = lax.broadcasted_iota(jnp.int32, (full, full), 0)
        cols_at = lax.broadcasted_iota(jnp.int32, (full, full), 1)

        def as_column(row):
            return jnp.sum(jnp.where(rows_at == cols_at, row, 0.0), axis=1, keepdims=True)

        weights = [
            decay(gates[head : head + 1, :], gates[heads + head : heads + head + 1, :], length, qk**-0.5)
            for head in range(heads)
        ]
        each = range(heads)
        loaded = []
        for head in each:
            first = slice(head * qk, (head + 1) * qk)
            second = slice(wq + head * vw, wq + (head + 1) * vw)
            of_wide, of_thin = (wide_ref[:, first], wide_ref[:, second]), (thin[:, first], thin[:, second])
            loaded.append(of_wide + of_thin if side == 0 else of_thin + of_wide)
        weights = [weight[:, :size] if side == 0 else weight[size:, :] for weight in weights]
        scores = [dot(q, k, NT) for q, g, k, v in loaded]
        pulled = [dot(g, v, NT) for q, g, k, v in loaded]
        scores = [scores[head] * weights[head] for head in each]
        norms = [jnp.sum(scores[head], axis=1, keepdims=True) for head in each]
        alongs = [jnp.sum(scores[head] * pulled[head], axis=1, keepdims=True) for head in each]
        if side == 0:
            at = chunk * heads
            norms = [norms[head] + as_column(stats_ref[at + head : at + head + 1, :]) for head in each]
            at += 2 * heads
            alongs = [alongs[head] + as_column(stats_ref[at + head : at + head + 1, :]) for head in each]
        terms = [backward_terms(norms[head], alongs[head]) for head in each]
        grad_scores = [pulled[head] * terms[head][0] + terms[head][1] for head in each]
        scaled = [scores[head] * terms[head][0] for head in each]
        grad_raw = [grad_scores[head] * weights[head] for head in each]
        turned = [(scaled[head].T, grad_raw[head].T) for head in each]
        if side == 0:
            scaled, grad_raw = [value[:size] for value in scaled], [value[:size] for value in grad_raw]
        else:
            turned = [(one[size:], other[size:]) for one, other in turned]
        sections = ((0, qk), (wq, qk), (2 * wq, vw), (2 * wq + wv, vw))
        for section, (start, step) in enumerate(sections):
            for head in each:
                q, g, k, v = loaded[head]
                left, right = (
                    (grad_raw[head], k), (turned[head][1], q), (turned[head][0], g), (scaled[head], v)
                )[section]
                value = wide_dot(left, right, NN).astype(jnp.bfloat16)
                result_ref[:, start + head * step : start + (head + 1) * step] = value
        for head in each:
            by_column = jnp.sum(grad_scores[head] * scores[head], axis=0, keepdims=True)
            by_row = terms[head][2]
            forget = gates[heads + head : heads + head + 1, :]
            live = cols_at[:1] < length
            slope = jnp.where(live, 1.0 / (1.0 + jnp.exp(forget)), 0.0)
            if side == 0 and chunk == 0:
                small_rows, small_cols = rows_at[:size, :size], cols_at[:size, :size]
                column = jnp.sum(jnp.where(small_rows == small_cols, by_column, 0.0), axis=1, keepdims=True)
                before = jnp.where(small_rows < small_cols, column - by_row[:size], 0.0)
                grad_log = jnp.sum(before, axis=0, keepdims=True)
                gates_ref[head : head + 1, :size] = by_column
                gates_ref[heads + head : heads + head + 1, :size] = grad_log * slope[:, :size]
            if side == 1:
                row = jnp.sum(jnp.where(rows_at[size:] == cols_at[size:], by_row, 0.0), axis=0, keepdims=True)
                if chunk == 1:
                    by_column = by_column + stats_ref[head : head + 1, :]
                    row = row + stats_ref[heads + head : heads + head + 1, :]
                    seen = jnp.full((1, full), True)
                else:
                    seen = cols_at[:1] >= size
                by_column = jnp.where(seen, by_column, 0.0)
                moved = as_column(row - by_column)
                grad_log = jnp.sum(jnp.where(rows_at >= cols_at, moved, 0.0), axis=0, keepdims=True)
                gates_ref[head : head + 1, :] = by_column
                gates_ref[heads + head : heads + head + 1, :] = jnp.where(seen, grad_log * slope, 0.0)
        theirs_ref[...] = result_ref[pl.ds(pl.multiple_of((1 - core) * rows, rows), rows), :]

    @pl.when(chip == 0)
    def _():
        part(0)

    @pl.when(chip != 0)
    def _():
        part(1)

    for copy in writes:
        copy.wait()


def merge_kernel(result_b, got_a, gates_a, gates_got, gates_b, *refs):
    *outputs, gi_ref, gf_ref, gates_ref, sems = refs[4:]
    chip, core = place()
    rows = got_a.shape[0]
    heads = gi_ref.shape[0]
    mine = result_b.at[pl.ds(pl.multiple_of(core * rows, rows), rows), :]
    copies = run_copies(placed(mine, outputs, 1, core) + placed(got_a, outputs, 0, 1 - core), sems)
    gates = jnp.where(chip == 0, gates_a[...] + gates_got[...], gates_b[...])
    gates_ref[0] = gates[:heads]
    gates_ref[1] = gates[heads:]
    copies += run_copies([(gates_ref.at[0], gi_ref), (gates_ref.at[1], gf_ref)], sems.at[pl.ds(8, 2)])
    for copy in copies:
        copy.wait()


def last_kernel(got_b, *refs):
    *outputs, sems = refs[4:]
    for copy in run_copies(placed(got_b, outputs, 1, 1 - place()[1]), sems):
        copy.wait()


def split_shards(queries, keys, values, cotangent, igate, fgate, lengths):
    rows = queries.shape[0]
    heads = igate.shape[0]
    qk = queries.shape[1] // (4 * heads)
    vw = values.shape[1] // (4 * heads)
    width = heads * (qk + vw)
    bf16, f32 = jnp.bfloat16, jnp.float32
    shape = jax.ShapeDtypeStruct
    vmem = pl.BlockSpec(memory_space=pltpu.VMEM)
    smem = pl.BlockSpec(memory_space=pltpu.SMEM)
    hbm = pl.BlockSpec(memory_space=pltpu.HBM)
    params = pltpu.CompilerParams(vmem_limit_bytes=32 * 1024 * 1024)
    costly = pl.CostEstimate(flops=4 * 10**10, bytes_accessed=0, transcendentals=0)
    dma = pltpu.SemaphoreType.DMA

    def swap(value, mask):
        return lax.ppermute(value, "head", [(s, s ^ mask) for s in range(4)])

    slots = igate.shape[1]
    gates_shape = shape((2 * heads, slots), f32)
    arrays = [pltpu.with_memory_space_constraint(a, pltpu.HBM) for a in (queries, keys, values, cotangent, igate, fgate)]
    cross_shape = shape((rows, width), bf16)
    a2_sent, d, to_core, gates = pl.pallas_call(
        pack_kernel,
        out_shape=(cross_shape, shape((rows, 2 * width), bf16), shape((rows, 4 * width), bf16), gates_shape),
        in_specs=[hbm] * 6,
        out_specs=(vmem,) * 4,
        scratch_shapes=[pltpu.VMEM(igate.shape, f32), pltpu.VMEM(igate.shape, f32), dma((16,))],
        compiler_params=params,
    )(*arrays)
    b2_sent, rest = pl.pallas_call(
        rest_kernel,
        out_shape=(cross_shape, shape((2, rows, width), bf16)),
        in_specs=[hbm] * 4,
        out_specs=(vmem,) * 2,
        scratch_shapes=[dma((6,))],
        compiler_params=params,
    )(*arrays[:4])
    from_core = swap(to_core, 1)
    gates_got = swap(gates, 2)
    a2, d = swap(a2_sent, 2), swap(d, 3)
    a2, gates_got = lax.optimization_barrier((a2, gates_got))
    both = shape((2, 2 * rows, width), bf16)
    qg, kv, stats = pl.pallas_call(
        functools.partial(local_kernel, qk, vw),
        out_shape=(both, both, shape((4 * heads, slots), f32)),
        in_specs=[smem] + [vmem] * 6,
        out_specs=(vmem,) * 3,
        cost_estimate=costly,
        compiler_params=params,
    )(lengths, a2_sent, b2_sent, rest, from_core, gates, gates_got)
    stats = swap(stats, 2)
    b2 = swap(b2_sent, 2)
    out_shape = tuple(shape(a.shape, bf16) for a in (queries, keys, values, values))

    def cross(chunk, received, written):
        return pl.pallas_call(
            functools.partial(cross_kernel, chunk, qk, vw),
            out_shape=(shape((2 * rows, 2 * width), bf16), shape((rows, 2 * width), bf16), gates_shape)
            + (out_shape if written else ()),
            in_specs=[smem] + [vmem] * (7 + len(written)),
            out_specs=(vmem,) * 3 + ((hbm,) * 4 if written else ()),
            scratch_shapes=[pltpu.VMEM((4 * rows, width), bf16)] + ([dma((4,))] if written else []),
            cost_estimate=costly,
            compiler_params=params,
        )(lengths, qg, kv, gates, gates_got, stats, *received, *written)

    result_a, theirs_a, gates_a = cross(0, (a2, d), ())
    gates_back = swap(gates_a, 2)
    got_a = swap(theirs_a, 1)
    result_b, theirs_b, gates_b, *outputs = cross(1, (b2, d), (result_a,))
    got_b = swap(theirs_b, 1)
    gate_shape = shape(igate.shape, f32)
    *outputs, grad_in, grad_forget = pl.pallas_call(
        merge_kernel,
        out_shape=out_shape + (gate_shape, gate_shape),
        in_specs=[vmem] * 5 + [hbm] * 4,
        out_specs=(hbm,) * 6,
        scratch_shapes=[pltpu.VMEM((2, *igate.shape), f32), dma((10,))],
        cost_estimate=costly,
        input_output_aliases={5: 0, 6: 1, 7: 2, 8: 3},
        compiler_params=params,
    )(result_b, got_a, gates_a, gates_back, gates_b, *outputs)
    gq, gk, gv, hidden = pl.pallas_call(
        last_kernel,
        out_shape=out_shape,
        in_specs=[vmem] + [hbm] * 4,
        out_specs=(hbm,) * 4,
        scratch_shapes=[dma((4,))],
        input_output_aliases={1: 0, 2: 1, 3: 2, 4: 3},
        compiler_params=params,
    )(got_b, *outputs)
    return hidden, gq, gk, gv, grad_in, grad_forget


def shards(*arrays):
    if lax.axis_size("head") == 4:
        return split_shards(*arrays)
    return swapped_shards(*arrays)


def solution(mesh):
    rows = P(("groups", "seq", "head"), None)
    gates = P("head", ("groups", "seq"))
    return jax.shard_map(
        shards,
        mesh=mesh,
        in_specs=(rows, rows, rows, rows, gates, gates, P(("groups", "seq"))),
        out_specs=(rows, rows, rows, rows, gates, gates),
        check_vma=False,
    )
```

```python
import functools

import jax
import jax.numpy as jnp
from jax import lax
from jax.experimental import pallas as pl
from jax.experimental.pallas import tpu as pltpu
from jax.sharding import PartitionSpec as P

FAR = -1e30


def dot(left, right, contract):
    return lax.dot_general(left, right, (contract, ((), ())), preferred_element_type=jnp.float32)


def halves(value):
    high = value.astype(jnp.bfloat16)
    return high, (value - high.astype(jnp.float32)).astype(jnp.bfloat16)


def wide_dot(left, right, contract):
    rows = left.shape[0]
    both = dot(jnp.concatenate(halves(left), axis=0), right, contract)
    return both[:rows] + both[rows:]


NN = ((1,), (0,))
NT = ((1,), (1,))
TN = ((0,), (0,))


def log_sigmoid(value):
    return jnp.minimum(value, 0.0) - jnp.log(1.0 + jnp.exp(-jnp.abs(value)))


def decay(in_gate, forget_gate, length, scale):
    size = in_gate.shape[1]
    rows = lax.broadcasted_iota(jnp.int32, (size, size), 0)
    cols = lax.broadcasted_iota(jnp.int32, (size, size), 1)
    logs = jnp.where(cols[:1] < length, log_sigmoid(forget_gate), 0.0)
    total_col = jnp.sum(jnp.where(cols <= rows, logs, 0.0), axis=1, keepdims=True)
    total_row = jnp.sum(jnp.where(cols == rows, total_col, 0.0), axis=0, keepdims=True)
    mask = (cols <= rows) & (rows < length)
    return jnp.exp(jnp.where(mask, total_col - total_row, FAR)) * (jnp.exp(in_gate) * scale)


def whole_kernel(heads, qk, vw, length_ref, x_ref, ig_ref, fg_ref, out_ref, gi_ref, gf_ref):
    length = length_ref[0]
    size = x_ref.shape[0]
    rows = lax.broadcasted_iota(jnp.int32, (size, size), 0)
    cols = lax.broadcasted_iota(jnp.int32, (size, size), 1)
    for head in range(heads):
        q = x_ref[:, head * qk : (head + 1) * qk]
        k = x_ref[:, (heads + head) * qk : (heads + head + 1) * qk]
        v0 = 2 * heads * qk + head * vw
        g0 = v0 + heads * vw
        v = x_ref[:, v0 : v0 + vw]
        g = x_ref[:, g0 : g0 + vw]
        forget = fg_ref[head : head + 1, :]
        weight = decay(ig_ref[head : head + 1, :], forget, length, qk**-0.5)
        scores = dot(q, k, NT) * weight
        pulled = dot(g, v, NT)
        norm = jnp.sum(scores, axis=1, keepdims=True)
        along = jnp.sum(scores * pulled, axis=1, keepdims=True)
        size_of = jnp.abs(norm)
        inverse = 1.0 / jnp.maximum(size_of, 1.0)
        share = jnp.where(size_of > 1.0, 1.0, jnp.where(size_of == 1.0, 0.5, 0.0))
        grad_norm = -along * inverse * inverse * share * jnp.where(norm < 0.0, -1.0, 1.0)
        grad_scores = pulled * inverse + grad_norm
        hidden = wide_dot(scores * inverse, v, NN)
        grad_raw = grad_scores * weight
        gq = wide_dot(grad_raw, k, NN)
        gk = wide_dot(grad_raw.T, q, NN)
        gv = wide_dot((scores * inverse).T, g, NN)
        out_ref[:, head * qk : (head + 1) * qk] = gq.astype(jnp.bfloat16)
        out_ref[:, (heads + head) * qk : (heads + head + 1) * qk] = gk.astype(jnp.bfloat16)
        out_ref[:, v0 : v0 + vw] = gv.astype(jnp.bfloat16)
        out_ref[:, g0 : g0 + vw] = hidden.astype(jnp.bfloat16)
        by_column = jnp.sum(grad_scores * scores, axis=0, keepdims=True)
        by_row = along * inverse * (1.0 - share)
        moved = by_row - jnp.sum(jnp.where(rows == cols, by_column, 0.0), axis=1, keepdims=True)
        grad_log = jnp.sum(jnp.where(rows >= cols, moved, 0.0), axis=0, keepdims=True)
        gi_ref[head : head + 1, :] = by_column
        gf_ref[head : head + 1, :] = jnp.where(
            cols[:1] < length, grad_log / (1.0 + jnp.exp(forget)), 0.0
        )


def swapped_shards(queries, keys, values, cotangent, igate, fgate, lengths):
    devices = lax.axis_size("head")
    rows = queries.shape[0]
    heads = igate.shape[0]
    qk = queries.shape[1] // (devices * heads)
    vw = values.shape[1] // (devices * heads)
    parts = [a.reshape(rows, devices, -1) for a in (queries, keys, values, cotangent)]
    joined = jnp.concatenate(parts, axis=2)
    here = lax.all_to_all(joined, "head", split_axis=1, concat_axis=0, tiled=True)
    here = here.reshape(rows * devices, -1)
    vmem = pl.BlockSpec(memory_space=pltpu.VMEM)
    out, grad_in, grad_forget = pl.pallas_call(
        functools.partial(whole_kernel, heads, qk, vw),
        out_shape=(
            jax.ShapeDtypeStruct(here.shape, jnp.bfloat16),
            jax.ShapeDtypeStruct(igate.shape, jnp.float32),
            jax.ShapeDtypeStruct(igate.shape, jnp.float32),
        ),
        in_specs=[pl.BlockSpec(memory_space=pltpu.SMEM), vmem, vmem, vmem],
        out_specs=(vmem, vmem, vmem),
        compiler_params=pltpu.CompilerParams(vmem_limit_bytes=32 * 1024 * 1024),
    )(lengths, here, igate, fgate)
    back = lax.all_to_all(
        out.reshape(devices, rows, -1), "head", split_axis=0, concat_axis=0, tiled=True
    )
    back = back.transpose(1, 0, 2)
    ends = [0, heads * qk, 2 * heads * qk, 2 * heads * qk + heads * vw, back.shape[2]]
    gq, gk, gv, hidden = [
        back[:, :, a:b].reshape(rows, -1) for a, b in zip(ends[:-1], ends[1:])
    ]
    return hidden, gq, gk, gv, grad_in, grad_forget


def backward_terms(norm, along):
    size = jnp.abs(norm)
    inverse = 1.0 / jnp.maximum(size, 1.0)
    share = jnp.where(size > 1.0, 1.0, jnp.where(size == 1.0, 0.5, 0.0))
    grad_norm = -along * inverse * inverse * share * jnp.where(norm < 0.0, -1.0, 1.0)
    return inverse, grad_norm, along * inverse * (1.0 - share)


def place():
    me = lax.axis_index("head")
    return me // 2, lax.rem(me, 2)


def run_copies(pairs, sems):
    copies = [pltpu.make_async_copy(a, b, sems.at[i]) for i, (a, b) in enumerate(pairs)]
    for copy in copies:
        copy.start()
    return copies


def block(ref, owner):
    width = ref.shape[1] // 4
    return ref.at[:, pl.ds(pl.multiple_of(owner * width, width), width)]


def block_copies(refs, owner, target):
    split = refs[0].shape[1] // 4
    end = split + refs[1].shape[1] // 4
    return [(block(refs[0], owner), target.at[:, :split]), (block(refs[1], owner), target.at[:, split:end])]


def copy_for_chip(moves, inputs, sems):
    q_ref, k_ref, v_ref, g_ref = inputs
    chip = place()[0]

    @pl.when(chip == 0)
    def _():
        run_copies(moves((k_ref, v_ref), (q_ref, g_ref)), sems)

    @pl.when(chip != 0)
    def _():
        run_copies(moves((q_ref, g_ref), (k_ref, v_ref)), sems)

    pairs = moves((k_ref, v_ref), (q_ref, g_ref))
    return [pltpu.make_async_copy(source, target, sems.at[i]) for i, (source, target) in enumerate(pairs)]


def pack_kernel(q_ref, k_ref, v_ref, g_ref, ig_ref, fg_ref, a2_ref, gates_ref, in_ref, out_ref, sems):
    core = place()[1]
    heads, slots = ig_ref.shape
    width = a2_ref.shape[1] - slots

    def moves(sent, kept):
        return [(ig_ref, in_ref), (fg_ref, out_ref)] + block_copies(sent, core, a2_ref)

    copies = copy_for_chip(moves, (q_ref, k_ref, v_ref, g_ref), sems)
    for copy in copies[:2]:
        copy.wait()
    gates_ref[:heads, :] = in_ref[...]
    gates_ref[heads:, :] = out_ref[...]
    gates = gates_ref[...]
    terms = []
    for _ in range(3):
        terms.append(gates.astype(jnp.bfloat16).astype(jnp.float32))
        gates = gates - terms[-1]
    terms.append(jnp.zeros((a2_ref.shape[0] - 6 * heads, slots), jnp.float32))
    a2_ref[:, width:] = jnp.concatenate(terms, axis=0).astype(jnp.bfloat16)
    for copy in copies[2:]:
        copy.wait()


def more_kernel(q_ref, k_ref, v_ref, g_ref, d_ref, m1_ref, sems):
    core = place()[1]
    width = m1_ref.shape[1] // 4

    def moves(sent, kept):
        pairs = []
        for chunk in range(2):
            pairs += block_copies(sent, 2 * chunk + 1 - core, d_ref.at[:, chunk * width : (chunk + 1) * width])
            for i, refs in enumerate((sent, kept)):
                start = (2 * chunk + i) * width
                pairs += block_copies(refs, 2 * chunk + 1 - core, m1_ref.at[:, start : start + width])
        return pairs

    for copy in copy_for_chip(moves, (q_ref, k_ref, v_ref, g_ref), sems):
        copy.wait()


def rest_kernel(q_ref, k_ref, v_ref, g_ref, b2_ref, rest_ref, sems):
    core = place()[1]

    def moves(sent, kept):
        pairs = block_copies(sent, 2 + core, b2_ref)
        return pairs + block_copies(kept, core, rest_ref.at[0]) + block_copies(kept, 2 + core, rest_ref.at[1])

    for copy in copy_for_chip(moves, (q_ref, k_ref, v_ref, g_ref), sems):
        copy.wait()


def join_kernel(a2_got, got_ref):
    count, slots = got_ref.shape
    terms = a2_got[:, a2_got.shape[1] - slots :].astype(jnp.float32)
    got_ref[...] = terms[:count] + terms[count : 2 * count] + terms[2 * count : 3 * count]


def local_kernel(
    qk, vw, length_ref, a2_ref, b2_ref, rest_ref, m1_ref, own_ref, got_ref, qg_ref, kv_ref, stats_ref
):
    chip, core = place()
    rows = m1_ref.shape[0]
    heads = own_ref.shape[0] // 2
    wq, wv = heads * qk, heads * vw
    width = wq + wv
    mine = pl.ds(pl.multiple_of(core * rows, rows), rows)
    theirs = pl.ds(pl.multiple_of((1 - core) * rows, rows), rows)

    def gather(sent, kept):
        for chunk, own in enumerate((a2_ref, b2_ref)):
            start = chunk * 2 * width
            sent[chunk, mine, :] = own[:, :width]
            sent[chunk, theirs, :] = m1_ref[:, start : start + width]
            kept[chunk, mine, :] = rest_ref[chunk]
            kept[chunk, theirs, :] = m1_ref[:, start + width : start + 2 * width]

    stats_ref[...] = jnp.zeros_like(stats_ref)
    length = length_ref[0]

    def part(side, chunks):
        size = 2 * rows
        low = side * size
        items = [(chunk, head) for chunk in chunks for head in range(heads)]
        scores, pulled = [], []
        for chunk, head in items:
            first = slice(head * qk, (head + 1) * qk)
            second = slice(wq + head * vw, wq + (head + 1) * vw)
            scores.append(dot(qg_ref[chunk, :, first], kv_ref[chunk, :, first], NT))
            pulled.append(dot(qg_ref[chunk, :, second], kv_ref[chunk, :, second], NT))
        for i, (chunk, head) in enumerate(items):
            gates = own_ref if side == chunk else got_ref
            weight = decay(gates[head : head + 1, :], gates[heads + head : heads + head + 1, :], length, qk**-0.5)
            scores[i] = scores[i] * weight[low : low + size, low : low + size]
        norms = [jnp.sum(score, axis=1, keepdims=True) for score in scores]
        alongs = [jnp.sum(score * pull, axis=1, keepdims=True) for score, pull in zip(scores, pulled)]
        on = lax.broadcasted_iota(jnp.int32, (size, 2 * size), 0) + low == lax.broadcasted_iota(
            jnp.int32, (size, 2 * size), 1
        )

        def as_row(column):
            return jnp.sum(jnp.where(on, column, 0.0), axis=0, keepdims=True)

        for (chunk, head), score, pull, norm, along in zip(items, scores, pulled, norms, alongs):
            if side == 1:
                at = chunk * heads + head
                stats_ref[at : at + 1, :] = as_row(norm)
                stats_ref[2 * heads + at : 2 * heads + at + 1, :] = as_row(along)
            else:
                inverse, grad_norm, by_row = backward_terms(norm, along)
                by_column = jnp.sum((pull * inverse + grad_norm) * score, axis=0, keepdims=True)
                stats_ref[head : head + 1, :size] = by_column
                stats_ref[heads + head : heads + head + 1, :] = as_row(by_row)

    @pl.when(chip == 0)
    def _():
        gather(kv_ref, qg_ref)
        part(0, (1,))

    @pl.when(chip != 0)
    def _():
        gather(qg_ref, kv_ref)
        part(1, (0, 1))


def placed(source, targets, chunk, by):
    pairs = []
    start = 0
    for target in targets:
        width = target.shape[1] // 4
        at = pl.ds(pl.multiple_of((2 * chunk + by) * width, width), width)
        pairs.append((source.at[:, start : start + width], target.at[:, at]))
        start += width
    return pairs


def cross_kernel(
    chunk, qk, vw, length_ref, qg_ref, kv_ref, own_ref, got_ref, stats_ref, same_ref, other_ref, *refs
):
    chip, core = place()
    writes = []
    if chunk == 0:
        result_ref, theirs_ref, gates_ref, wide_ref = refs
    else:
        result_a, result_ref, theirs_ref, gates_ref, *outputs, wide_ref, sems = refs
        rows = theirs_ref.shape[0]
        mine_a = result_a.at[pl.ds(pl.multiple_of(core * rows, rows), rows), :]
        writes = run_copies(placed(mine_a, outputs, 0, core), sems)
    rows = theirs_ref.shape[0]
    size = 2 * rows
    heads = own_ref.shape[0] // 2
    wq, wv = heads * qk, heads * vw

    def gather(side, local):
        base = 0 if side else size
        wide_ref[side * size : (side + 1) * size, :] = local[chunk]
        for ref, by in ((same_ref, core), (other_ref, 1 - core)):
            start = chunk * (wq + wv) if ref is other_ref else 0
            wide_ref[pl.ds(pl.multiple_of(base + by * rows, rows), rows), :] = ref[:, start : start + wq + wv]

    length = length_ref[0]
    gates_ref[...] = jnp.zeros_like(gates_ref)

    def part(side):
        gather(side, kv_ref if side else qg_ref)
        thin = (qg_ref if side else kv_ref).at[chunk]
        gates = own_ref if side == chunk else got_ref
        full = 2 * size
        rows_at = lax.broadcasted_iota(jnp.int32, (full, full), 0)
        cols_at = lax.broadcasted_iota(jnp.int32, (full, full), 1)

        def as_column(row):
            return jnp.sum(jnp.where(rows_at == cols_at, row, 0.0), axis=1, keepdims=True)

        weights = [
            decay(gates[head : head + 1, :], gates[heads + head : heads + head + 1, :], length, qk**-0.5)
            for head in range(heads)
        ]
        each = range(heads)
        loaded = []
        for head in each:
            first = slice(head * qk, (head + 1) * qk)
            second = slice(wq + head * vw, wq + (head + 1) * vw)
            of_wide, of_thin = (wide_ref[:, first], wide_ref[:, second]), (thin[:, first], thin[:, second])
            loaded.append(of_wide + of_thin if side == 0 else of_thin + of_wide)
        weights = [weight[:, :size] if side == 0 else weight[size:, :] for weight in weights]
        scores = [dot(q, k, NT) for q, g, k, v in loaded]
        pulled = [dot(g, v, NT) for q, g, k, v in loaded]
        scores = [scores[head] * weights[head] for head in each]
        norms = [jnp.sum(scores[head], axis=1, keepdims=True) for head in each]
        alongs = [jnp.sum(scores[head] * pulled[head], axis=1, keepdims=True) for head in each]
        if side == 0:
            at = chunk * heads
            norms = [norms[head] + as_column(stats_ref[at + head : at + head + 1, :]) for head in each]
            at += 2 * heads
            alongs = [alongs[head] + as_column(stats_ref[at + head : at + head + 1, :]) for head in each]
        terms = [backward_terms(norms[head], alongs[head]) for head in each]
        grad_scores = [pulled[head] * terms[head][0] + terms[head][1] for head in each]
        scaled = [scores[head] * terms[head][0] for head in each]
        grad_raw = [grad_scores[head] * weights[head] for head in each]
        turned = [(scaled[head].T, grad_raw[head].T) for head in each]
        if side == 0:
            scaled, grad_raw = [value[:size] for value in scaled], [value[:size] for value in grad_raw]
        else:
            turned = [(one[size:], other[size:]) for one, other in turned]
        sections = ((0, qk), (wq, qk), (2 * wq, vw), (2 * wq + wv, vw))
        for section, (start, step) in enumerate(sections):
            for head in each:
                q, g, k, v = loaded[head]
                left, right = (
                    (grad_raw[head], k), (turned[head][1], q), (turned[head][0], g), (scaled[head], v)
                )[section]
                value = wide_dot(left, right, NN).astype(jnp.bfloat16)
                result_ref[:, start + head * step : start + (head + 1) * step] = value
        for head in each:
            by_column = jnp.sum(grad_scores[head] * scores[head], axis=0, keepdims=True)
            by_row = terms[head][2]
            forget = gates[heads + head : heads + head + 1, :]
            live = cols_at[:1] < length
            slope = jnp.where(live, 1.0 / (1.0 + jnp.exp(forget)), 0.0)
            if side == 0 and chunk == 0:
                small_rows, small_cols = rows_at[:size, :size], cols_at[:size, :size]
                column = jnp.sum(jnp.where(small_rows == small_cols, by_column, 0.0), axis=1, keepdims=True)
                before = jnp.where(small_rows < small_cols, column - by_row[:size], 0.0)
                grad_log = jnp.sum(before, axis=0, keepdims=True)
                gates_ref[head : head + 1, :size] = by_column
                gates_ref[heads + head : heads + head + 1, :size] = grad_log * slope[:, :size]
            if side == 1:
                row = jnp.sum(jnp.where(rows_at[size:] == cols_at[size:], by_row, 0.0), axis=0, keepdims=True)
                if chunk == 1:
                    by_column = by_column + stats_ref[head : head + 1, :]
                    row = row + stats_ref[heads + head : heads + head + 1, :]
                    seen = jnp.full((1, full), True)
                else:
                    seen = cols_at[:1] >= size
                by_column = jnp.where(seen, by_column, 0.0)
                moved = as_column(row - by_column)
                grad_log = jnp.sum(jnp.where(rows_at >= cols_at, moved, 0.0), axis=0, keepdims=True)
                gates_ref[head : head + 1, :] = by_column
                gates_ref[heads + head : heads + head + 1, :] = jnp.where(seen, grad_log * slope, 0.0)
        theirs_ref[...] = result_ref[pl.ds(pl.multiple_of((1 - core) * rows, rows), rows), :]

    @pl.when(chip == 0)
    def _():
        part(0)

    @pl.when(chip != 0)
    def _():
        part(1)

    for copy in writes:
        copy.wait()


def hold_kernel(in_ref, out_ref):
    out_ref[...] = in_ref[...]


def merge_kernel(result_b, got_a, gates_in, *refs):
    *outputs, gates_ref, sems = refs[4:]
    core = place()[1]
    rows = got_a.shape[0]
    mine = result_b.at[pl.ds(pl.multiple_of(core * rows, rows), rows), :]
    copies = run_copies(placed(mine, outputs, 1, core) + placed(got_a, outputs, 0, 1 - core), sems)
    gates_ref[...] = gates_in[...]
    for copy in copies:
        copy.wait()


def gates_kernel(gates_a, gates_got, gates_b, gi_ref, gf_ref):
    heads = gi_ref.shape[0]
    gates = jnp.where(place()[0] == 0, gates_a[...] + gates_got[...], gates_b[...])
    gi_ref[...] = gates[:heads]
    gf_ref[...] = gates[heads:]


def last_kernel(got_b, gi_in, gf_in, *refs):
    *outputs, gi_ref, gf_ref, sems = refs[4:]
    pairs = placed(got_b, outputs, 1, 1 - place()[1]) + [(gi_in, gi_ref), (gf_in, gf_ref)]
    for copy in run_copies(pairs, sems):
        copy.wait()


def split_shards(queries, keys, values, cotangent, igate, fgate, lengths):
    rows = queries.shape[0]
    heads = igate.shape[0]
    qk = queries.shape[1] // (4 * heads)
    vw = values.shape[1] // (4 * heads)
    width = heads * (qk + vw)
    bf16, f32 = jnp.bfloat16, jnp.float32
    shape = jax.ShapeDtypeStruct
    vmem = pl.BlockSpec(memory_space=pltpu.VMEM)
    smem = pl.BlockSpec(memory_space=pltpu.SMEM)
    hbm = pl.BlockSpec(memory_space=pltpu.HBM)
    params = pltpu.CompilerParams(vmem_limit_bytes=32 * 1024 * 1024)

    def flops(count):
        return pl.CostEstimate(flops=count, bytes_accessed=0, transcendentals=0)

    costly = flops(4 * 10**10)
    dma = pltpu.SemaphoreType.DMA

    def swap(value, mask):
        return lax.ppermute(value, "head", [(s, s ^ mask) for s in range(4)])

    slots = igate.shape[1]
    gates_shape = shape((2 * heads, slots), f32)
    arrays = [pltpu.with_memory_space_constraint(a, pltpu.HBM) for a in (queries, keys, values, cotangent, igate, fgate)]
    cross_shape = shape((rows, width), bf16)
    a2_sent, gates = pl.pallas_call(
        pack_kernel,
        out_shape=(shape((rows, width + slots), bf16), gates_shape),
        in_specs=[hbm] * 6,
        out_specs=(vmem,) * 2,
        scratch_shapes=[pltpu.VMEM(igate.shape, f32), pltpu.VMEM(igate.shape, f32), dma((4,))],
        compiler_params=params,
    )(*arrays)
    a2 = swap(a2_sent, 2)
    d, to_core = pl.pallas_call(
        more_kernel,
        out_shape=(shape((rows, 2 * width), bf16), shape((rows, 4 * width), bf16)),
        in_specs=[hbm] * 4,
        out_specs=(vmem,) * 2,
        scratch_shapes=[dma((12,))],
        compiler_params=params,
    )(*arrays[:4])
    b2_sent, rest = pl.pallas_call(
        rest_kernel,
        out_shape=(cross_shape, shape((2, rows, width), bf16)),
        in_specs=[hbm] * 4,
        out_specs=(vmem,) * 2,
        scratch_shapes=[dma((6,))],
        compiler_params=params,
    )(*arrays[:4])
    from_core = swap(to_core, 1)
    d = swap(d, 3)
    gates_got = pl.pallas_call(
        join_kernel,
        out_shape=gates_shape,
        in_specs=[vmem],
        out_specs=vmem,
        cost_estimate=costly,
        compiler_params=params,
    )(a2)
    both = shape((2, 2 * rows, width), bf16)
    qg, kv, stats = pl.pallas_call(
        functools.partial(local_kernel, qk, vw),
        out_shape=(both, both, shape((4 * heads, slots), f32)),
        in_specs=[smem] + [vmem] * 6,
        out_specs=(vmem,) * 3,
        cost_estimate=costly,
        compiler_params=params,
    )(lengths, a2_sent, b2_sent, rest, from_core, gates, gates_got)
    stats = swap(stats, 2)
    b2 = swap(b2_sent, 2)
    out_shape = tuple(shape(a.shape, bf16) for a in (queries, keys, values, values))

    def cross(chunk, received, written):
        return pl.pallas_call(
            functools.partial(cross_kernel, chunk, qk, vw),
            out_shape=(shape((2 * rows, 2 * width), bf16), shape((rows, 2 * width), bf16), gates_shape)
            + (out_shape if written else ()),
            in_specs=[smem] + [vmem] * (7 + len(written)),
            out_specs=(vmem,) * 3 + ((hbm,) * 4 if written else ()),
            scratch_shapes=[pltpu.VMEM((4 * rows, width), bf16)] + ([dma((4,))] if written else []),
            cost_estimate=flops(2 * 10**9) if written else costly,
            compiler_params=params,
        )(lengths, qg, kv, gates, gates_got, stats, *received, *written)

    result_a, theirs_a, gates_a = cross(0, (a2, d), ())
    gates_a = pl.pallas_call(
        hold_kernel,
        out_shape=gates_shape,
        in_specs=[vmem],
        out_specs=vmem,
        cost_estimate=flops(0),
        compiler_params=params,
    )(gates_a)
    gates_back = swap(gates_a, 2)
    got_a = swap(theirs_a, 1)
    result_b, theirs_b, gates_b, *outputs = cross(1, (b2, d), (result_a,))
    theirs_b, got_a = lax.optimization_barrier((theirs_b, got_a))
    got_b = swap(theirs_b, 1)
    *outputs, gates_b = pl.pallas_call(
        merge_kernel,
        out_shape=out_shape + (gates_shape,),
        in_specs=[vmem] * 3 + [hbm] * 4,
        out_specs=(hbm,) * 4 + (vmem,),
        scratch_shapes=[dma((8,))],
        input_output_aliases={3: 0, 4: 1, 5: 2, 6: 3},
        cost_estimate=flops(0),
        compiler_params=params,
    )(result_b, got_a, gates_b, *outputs)
    gate_shape = shape(igate.shape, f32)
    gate_grads = pl.pallas_call(
        gates_kernel,
        out_shape=(gate_shape, gate_shape),
        in_specs=[vmem] * 3,
        out_specs=(vmem,) * 2,
        cost_estimate=costly,
        compiler_params=params,
    )(gates_a, gates_back, gates_b)
    gq, gk, gv, hidden, grad_in, grad_forget = pl.pallas_call(
        last_kernel,
        out_shape=out_shape + (gate_shape, gate_shape),
        in_specs=[vmem] * 3 + [hbm] * 4,
        out_specs=(hbm,) * 6,
        scratch_shapes=[dma((6,))],
        input_output_aliases={3: 0, 4: 1, 5: 2, 6: 3},
        compiler_params=params,
    )(got_b, *gate_grads, *outputs)
    return hidden, gq, gk, gv, grad_in, grad_forget


def shards(*arrays):
    if lax.axis_size("head") == 4:
        return split_shards(*arrays)
    return swapped_shards(*arrays)


def solution(mesh):
    rows = P(("groups", "seq", "head"), None)
    gates = P("head", ("groups", "seq"))
    return jax.shard_map(
        shards,
        mesh=mesh,
        in_specs=(rows, rows, rows, rows, gates, gates, P(("groups", "seq"))),
        out_specs=(rows, rows, rows, rows, gates, gates),
        check_vma=False,
    )
```

```python
import functools

import jax
import jax.numpy as jnp
from jax import lax
from jax.experimental import pallas as pl
from jax.experimental.pallas import tpu as pltpu
from jax.sharding import PartitionSpec as P

FAR = -1e30


def dot(left, right, contract):
    return lax.dot_general(left, right, (contract, ((), ())), preferred_element_type=jnp.float32)


def halves(value):
    high = value.astype(jnp.bfloat16)
    return high, (value - high.astype(jnp.float32)).astype(jnp.bfloat16)


def wide_dot(left, right, contract):
    rows = left.shape[0]
    both = dot(jnp.concatenate(halves(left), axis=0), right, contract)
    return both[:rows] + both[rows:]


NN = ((1,), (0,))
NT = ((1,), (1,))
TN = ((0,), (0,))


def log_sigmoid(value):
    return jnp.minimum(value, 0.0) - jnp.log(1.0 + jnp.exp(-jnp.abs(value)))


def decay(in_gate, forget_gate, length, scale):
    size = in_gate.shape[1]
    rows = lax.broadcasted_iota(jnp.int32, (size, size), 0)
    cols = lax.broadcasted_iota(jnp.int32, (size, size), 1)
    logs = jnp.where(cols[:1] < length, log_sigmoid(forget_gate), 0.0)
    total_col = jnp.sum(jnp.where(cols <= rows, logs, 0.0), axis=1, keepdims=True)
    total_row = jnp.sum(jnp.where(cols == rows, total_col, 0.0), axis=0, keepdims=True)
    mask = (cols <= rows) & (rows < length)
    return jnp.exp(jnp.where(mask, total_col - total_row, FAR)) * (jnp.exp(in_gate) * scale)


def whole_kernel(heads, qk, vw, length_ref, x_ref, ig_ref, fg_ref, out_ref, gi_ref, gf_ref):
    length = length_ref[0]
    size = x_ref.shape[0]
    rows = lax.broadcasted_iota(jnp.int32, (size, size), 0)
    cols = lax.broadcasted_iota(jnp.int32, (size, size), 1)
    for head in range(heads):
        q = x_ref[:, head * qk : (head + 1) * qk]
        k = x_ref[:, (heads + head) * qk : (heads + head + 1) * qk]
        v0 = 2 * heads * qk + head * vw
        g0 = v0 + heads * vw
        v = x_ref[:, v0 : v0 + vw]
        g = x_ref[:, g0 : g0 + vw]
        forget = fg_ref[head : head + 1, :]
        weight = decay(ig_ref[head : head + 1, :], forget, length, qk**-0.5)
        scores = dot(q, k, NT) * weight
        pulled = dot(g, v, NT)
        norm = jnp.sum(scores, axis=1, keepdims=True)
        along = jnp.sum(scores * pulled, axis=1, keepdims=True)
        size_of = jnp.abs(norm)
        inverse = 1.0 / jnp.maximum(size_of, 1.0)
        share = jnp.where(size_of > 1.0, 1.0, jnp.where(size_of == 1.0, 0.5, 0.0))
        grad_norm = -along * inverse * inverse * share * jnp.where(norm < 0.0, -1.0, 1.0)
        grad_scores = pulled * inverse + grad_norm
        hidden = wide_dot(scores * inverse, v, NN)
        grad_raw = grad_scores * weight
        gq = wide_dot(grad_raw, k, NN)
        gk = wide_dot(grad_raw.T, q, NN)
        gv = wide_dot((scores * inverse).T, g, NN)
        out_ref[:, head * qk : (head + 1) * qk] = gq.astype(jnp.bfloat16)
        out_ref[:, (heads + head) * qk : (heads + head + 1) * qk] = gk.astype(jnp.bfloat16)
        out_ref[:, v0 : v0 + vw] = gv.astype(jnp.bfloat16)
        out_ref[:, g0 : g0 + vw] = hidden.astype(jnp.bfloat16)
        by_column = jnp.sum(grad_scores * scores, axis=0, keepdims=True)
        by_row = along * inverse * (1.0 - share)
        moved = by_row - jnp.sum(jnp.where(rows == cols, by_column, 0.0), axis=1, keepdims=True)
        grad_log = jnp.sum(jnp.where(rows >= cols, moved, 0.0), axis=0, keepdims=True)
        gi_ref[head : head + 1, :] = by_column
        gf_ref[head : head + 1, :] = jnp.where(
            cols[:1] < length, grad_log / (1.0 + jnp.exp(forget)), 0.0
        )


def swapped_shards(queries, keys, values, cotangent, igate, fgate, lengths):
    devices = lax.axis_size("head")
    rows = queries.shape[0]
    heads = igate.shape[0]
    qk = queries.shape[1] // (devices * heads)
    vw = values.shape[1] // (devices * heads)
    parts = [a.reshape(rows, devices, -1) for a in (queries, keys, values, cotangent)]
    joined = jnp.concatenate(parts, axis=2)
    here = lax.all_to_all(joined, "head", split_axis=1, concat_axis=0, tiled=True)
    here = here.reshape(rows * devices, -1)
    vmem = pl.BlockSpec(memory_space=pltpu.VMEM)
    out, grad_in, grad_forget = pl.pallas_call(
        functools.partial(whole_kernel, heads, qk, vw),
        out_shape=(
            jax.ShapeDtypeStruct(here.shape, jnp.bfloat16),
            jax.ShapeDtypeStruct(igate.shape, jnp.float32),
            jax.ShapeDtypeStruct(igate.shape, jnp.float32),
        ),
        in_specs=[pl.BlockSpec(memory_space=pltpu.SMEM), vmem, vmem, vmem],
        out_specs=(vmem, vmem, vmem),
        compiler_params=pltpu.CompilerParams(vmem_limit_bytes=32 * 1024 * 1024),
    )(lengths, here, igate, fgate)
    back = lax.all_to_all(
        out.reshape(devices, rows, -1), "head", split_axis=0, concat_axis=0, tiled=True
    )
    back = back.transpose(1, 0, 2)
    ends = [0, heads * qk, 2 * heads * qk, 2 * heads * qk + heads * vw, back.shape[2]]
    gq, gk, gv, hidden = [
        back[:, :, a:b].reshape(rows, -1) for a, b in zip(ends[:-1], ends[1:])
    ]
    return hidden, gq, gk, gv, grad_in, grad_forget


def backward_terms(norm, along):
    size = jnp.abs(norm)
    inverse = 1.0 / jnp.maximum(size, 1.0)
    share = jnp.where(size > 1.0, 1.0, jnp.where(size == 1.0, 0.5, 0.0))
    grad_norm = -along * inverse * inverse * share * jnp.where(norm < 0.0, -1.0, 1.0)
    return inverse, grad_norm, along * inverse * (1.0 - share)


def place():
    me = lax.axis_index("head")
    return me // 2, lax.rem(me, 2)


def run_copies(pairs, sems):
    copies = [pltpu.make_async_copy(a, b, sems.at[i]) for i, (a, b) in enumerate(pairs)]
    for copy in copies:
        copy.start()
    return copies


def block(ref, owner):
    width = ref.shape[1] // 4
    return ref.at[:, pl.ds(pl.multiple_of(owner * width, width), width)]


def block_copies(refs, owner, target):
    split = refs[0].shape[1] // 4
    end = split + refs[1].shape[1] // 4
    return [(block(refs[0], owner), target.at[:, :split]), (block(refs[1], owner), target.at[:, split:end])]


def copy_for_chip(moves, inputs, sems):
    q_ref, k_ref, v_ref, g_ref = inputs
    chip = place()[0]

    @pl.when(chip == 0)
    def _():
        run_copies(moves((k_ref, v_ref), (q_ref, g_ref)), sems)

    @pl.when(chip != 0)
    def _():
        run_copies(moves((q_ref, g_ref), (k_ref, v_ref)), sems)

    pairs = moves((k_ref, v_ref), (q_ref, g_ref))
    return [pltpu.make_async_copy(source, target, sems.at[i]) for i, (source, target) in enumerate(pairs)]


def pack_kernel(q_ref, k_ref, v_ref, g_ref, ig_ref, fg_ref, a2_ref, gates_ref, in_ref, out_ref, sems):
    core = place()[1]
    heads, slots = ig_ref.shape
    width = a2_ref.shape[1] - slots

    def moves(sent, kept):
        return [(ig_ref, in_ref), (fg_ref, out_ref)] + block_copies(sent, core, a2_ref)

    copies = copy_for_chip(moves, (q_ref, k_ref, v_ref, g_ref), sems)
    for copy in copies[:2]:
        copy.wait()
    gates_ref[:heads, :] = in_ref[...]
    gates_ref[heads:, :] = out_ref[...]
    gates = gates_ref[...]
    terms = []
    for _ in range(3):
        terms.append(gates.astype(jnp.bfloat16).astype(jnp.float32))
        gates = gates - terms[-1]
    terms.append(jnp.zeros((a2_ref.shape[0] - 6 * heads, slots), jnp.float32))
    a2_ref[:, width:] = jnp.concatenate(terms, axis=0).astype(jnp.bfloat16)
    for copy in copies[2:]:
        copy.wait()


def more_kernel(q_ref, k_ref, v_ref, g_ref, d_ref, m1_ref, sems):
    core = place()[1]
    width = m1_ref.shape[1] // 4

    def moves(sent, kept):
        pairs = []
        for chunk in range(2):
            pairs += block_copies(sent, 2 * chunk + 1 - core, d_ref.at[:, chunk * width : (chunk + 1) * width])
            for i, refs in enumerate((sent, kept)):
                start = (2 * chunk + i) * width
                pairs += block_copies(refs, 2 * chunk + 1 - core, m1_ref.at[:, start : start + width])
        return pairs

    for copy in copy_for_chip(moves, (q_ref, k_ref, v_ref, g_ref), sems):
        copy.wait()


def rest_kernel(q_ref, k_ref, v_ref, g_ref, b2_ref, rest_ref, sems):
    core = place()[1]

    def moves(sent, kept):
        pairs = block_copies(sent, 2 + core, b2_ref)
        return pairs + block_copies(kept, core, rest_ref.at[0]) + block_copies(kept, 2 + core, rest_ref.at[1])

    for copy in copy_for_chip(moves, (q_ref, k_ref, v_ref, g_ref), sems):
        copy.wait()


def join_kernel(a2_got, got_ref):
    count, slots = got_ref.shape
    terms = a2_got[:, a2_got.shape[1] - slots :].astype(jnp.float32)
    got_ref[...] = terms[:count] + terms[count : 2 * count] + terms[2 * count : 3 * count]


def local_kernel(
    qk, vw, length_ref, a2_ref, b2_ref, rest_ref, m1_ref, own_ref, got_ref, qg_ref, kv_ref, stats_ref
):
    chip, core = place()
    rows = m1_ref.shape[0]
    heads = own_ref.shape[0] // 2
    wq, wv = heads * qk, heads * vw
    width = wq + wv
    mine = pl.ds(pl.multiple_of(core * rows, rows), rows)
    theirs = pl.ds(pl.multiple_of((1 - core) * rows, rows), rows)

    def gather(sent, kept):
        for chunk, own in enumerate((a2_ref, b2_ref)):
            start = chunk * 2 * width
            sent[chunk, mine, :] = own[:, :width]
            sent[chunk, theirs, :] = m1_ref[:, start : start + width]
            kept[chunk, mine, :] = rest_ref[chunk]
            kept[chunk, theirs, :] = m1_ref[:, start + width : start + 2 * width]

    stats_ref[...] = jnp.zeros_like(stats_ref)
    length = length_ref[0]

    def part(side, chunks):
        size = 2 * rows
        low = side * size
        items = [(chunk, head) for chunk in chunks for head in range(heads)]
        scores, pulled = [], []
        for chunk, head in items:
            first = slice(head * qk, (head + 1) * qk)
            second = slice(wq + head * vw, wq + (head + 1) * vw)
            scores.append(dot(qg_ref[chunk, :, first], kv_ref[chunk, :, first], NT))
            pulled.append(dot(qg_ref[chunk, :, second], kv_ref[chunk, :, second], NT))
        for i, (chunk, head) in enumerate(items):
            gates = own_ref if side == chunk else got_ref
            weight = decay(gates[head : head + 1, :], gates[heads + head : heads + head + 1, :], length, qk**-0.5)
            scores[i] = scores[i] * weight[low : low + size, low : low + size]
        norms = [jnp.sum(score, axis=1, keepdims=True) for score in scores]
        alongs = [jnp.sum(score * pull, axis=1, keepdims=True) for score, pull in zip(scores, pulled)]
        on = lax.broadcasted_iota(jnp.int32, (size, 2 * size), 0) + low == lax.broadcasted_iota(
            jnp.int32, (size, 2 * size), 1
        )

        def as_row(column):
            return jnp.sum(jnp.where(on, column, 0.0), axis=0, keepdims=True)

        for (chunk, head), score, pull, norm, along in zip(items, scores, pulled, norms, alongs):
            if side == 1:
                at = chunk * heads + head
                stats_ref[at : at + 1, :] = as_row(norm)
                stats_ref[2 * heads + at : 2 * heads + at + 1, :] = as_row(along)
            else:
                inverse, grad_norm, by_row = backward_terms(norm, along)
                by_column = jnp.sum((pull * inverse + grad_norm) * score, axis=0, keepdims=True)
                stats_ref[head : head + 1, :size] = by_column
                stats_ref[heads + head : heads + head + 1, :] = as_row(by_row)

    @pl.when(chip == 0)
    def _():
        gather(kv_ref, qg_ref)
        part(0, (1,))

    @pl.when(chip != 0)
    def _():
        gather(qg_ref, kv_ref)
        part(1, (0, 1))


def placed(source, targets, chunk, by):
    pairs = []
    start = 0
    for target in targets:
        width = target.shape[1] // 4
        at = pl.ds(pl.multiple_of((2 * chunk + by) * width, width), width)
        pairs.append((source.at[:, start : start + width], target.at[:, at]))
        start += width
    return pairs


def cross_kernel(
    chunk, sides, work, qk, vw, length_ref, qg_ref, kv_ref, own_ref, got_ref, same_ref, other_ref, *refs
):
    chip, core = place()
    rows_wanted, gates_wanted = work != "gates", work != "rows"
    if work == "gates":
        gates_ref, wide_ref = refs
    elif work == "rows":
        _, result_ref, theirs_ref, wide_ref = refs
    elif sides == (0,):
        stats_ref, *later, result_ref, theirs_ref, gates_ref, wide_ref = refs
    else:
        stats_ref, near_ref, share_ref, result_ref, theirs_ref, gates_ref, wide_ref = refs
    rows = other_ref.shape[0]
    size = 2 * rows
    heads = own_ref.shape[0] // 2
    wq, wv = heads * qk, heads * vw

    def gather(side, local):
        base = 0 if side else size
        if side == 1 or chunk == 0:
            wide_ref[side * size : (side + 1) * size, :] = local[chunk]
        for ref, by in ((same_ref, core), (other_ref, 1 - core)):
            start = chunk * (wq + wv) if ref is other_ref else 0
            wide_ref[pl.ds(pl.multiple_of(base + by * rows, rows), rows), :] = ref[:, start : start + wq + wv]

    length = length_ref[0]

    def part(side):
        if gates_wanted:
            gates_ref[...] = jnp.zeros_like(gates_ref)
        gather(side, kv_ref if side else qg_ref)
        thin = (qg_ref if side else kv_ref).at[chunk]
        gates = own_ref if side == chunk else got_ref
        full = 2 * size
        rows_at = lax.broadcasted_iota(jnp.int32, (full, full), 0)
        cols_at = lax.broadcasted_iota(jnp.int32, (full, full), 1)

        def as_column(row):
            return jnp.sum(jnp.where(rows_at == cols_at, row, 0.0), axis=1, keepdims=True)

        weights = [
            decay(gates[head : head + 1, :], gates[heads + head : heads + head + 1, :], length, qk**-0.5)
            for head in range(heads)
        ]
        each = range(heads)
        far = side == 0 and chunk == 1
        loaded = []
        for head in each:
            first = slice(head * qk, (head + 1) * qk)
            second = slice(wq + head * vw, wq + (head + 1) * vw)
            seen = slice(size, 2 * size) if far else slice(None)
            of_wide, of_thin = (wide_ref[seen, first], wide_ref[seen, second]), (thin[:, first], thin[:, second])
            loaded.append(of_wide + of_thin if side == 0 else of_thin + of_wide)
        weights = [weight[:, :size] if side == 0 else weight for weight in weights]
        weights = [weight[size:] if side == 1 or far else weight for weight in weights]
        scores = [dot(q, k, NT) for q, g, k, v in loaded]
        pulled = [dot(g, v, NT) for q, g, k, v in loaded]
        scores = [scores[head] * weights[head] for head in each]
        norms = [jnp.sum(scores[head], axis=1, keepdims=True) for head in each]
        alongs = [jnp.sum(scores[head] * pulled[head], axis=1, keepdims=True) for head in each]
        if side == 0:
            at = chunk * heads
            sums = [as_column(stats_ref[at + head : at + head + 1, :]) for head in each]
            norms = [norms[head] + (sums[head][size:] if far else sums[head]) for head in each]
            at += 2 * heads
            sums = [as_column(stats_ref[at + head : at + head + 1, :]) for head in each]
            alongs = [alongs[head] + (sums[head][size:] if far else sums[head]) for head in each]
        terms = [backward_terms(norms[head], alongs[head]) for head in each]
        grad_scores = [pulled[head] * terms[head][0] + terms[head][1] for head in each]
        if rows_wanted:
            scaled = [scores[head] * terms[head][0] for head in each]
            grad_raw = [grad_scores[head] * weights[head] for head in each]
            turned = [(scaled[head].T, grad_raw[head].T) for head in each]
            if far:
                pass
            elif side == 0:
                scaled, grad_raw = [value[:size] for value in scaled], [value[:size] for value in grad_raw]
            else:
                turned = [(one[size:], other[size:]) for one, other in turned]
            sections = ((0, qk), (wq, qk), (2 * wq, vw), (2 * wq + wv, vw))
            for section, (start, step) in enumerate(sections):
                for head in each:
                    columns = slice(start + head * step, start + (head + 1) * step)
                    if far and section in (0, 3):
                        at = (section // 3) * wq + head * step
                        result_ref[:, columns] = near_ref[:, at : at + step]
                        continue
                    q, g, k, v = loaded[head]
                    left, right = (
                        (grad_raw[head], k), (turned[head][1], q), (turned[head][0], g), (scaled[head], v)
                    )[section]
                    value = wide_dot(left, right, NN)
                    if far:
                        at = (section - 1) * wq + head * step
                        value = value + share_ref[:, at : at + step]
                    result_ref[:, columns] = value.astype(jnp.bfloat16)
        for head in each if gates_wanted else ():
            by_column = jnp.sum(grad_scores[head] * scores[head], axis=0, keepdims=True)
            by_row = terms[head][2]
            forget = gates[heads + head : heads + head + 1, :]
            live = cols_at[:1] < length
            slope = jnp.where(live, 1.0 / (1.0 + jnp.exp(forget)), 0.0)
            if side == 0 and chunk == 0:
                small_rows, small_cols = rows_at[:size, :size], cols_at[:size, :size]
                column = jnp.sum(jnp.where(small_rows == small_cols, by_column, 0.0), axis=1, keepdims=True)
                before = jnp.where(small_rows < small_cols, column - by_row[:size], 0.0)
                grad_log = jnp.sum(before, axis=0, keepdims=True)
                gates_ref[head : head + 1, :size] = by_column
                gates_ref[heads + head : heads + head + 1, :size] = grad_log * slope[:, :size]
            if side == 1:
                row = jnp.sum(jnp.where(rows_at[size:] == cols_at[size:], by_row, 0.0), axis=0, keepdims=True)
                if chunk == 1:
                    by_column = by_column + stats_ref[head : head + 1, :]
                    row = row + stats_ref[heads + head : heads + head + 1, :]
                    seen = jnp.full((1, full), True)
                else:
                    seen = cols_at[:1] >= size
                by_column = jnp.where(seen, by_column, 0.0)
                moved = as_column(row - by_column)
                grad_log = jnp.sum(jnp.where(rows_at >= cols_at, moved, 0.0), axis=0, keepdims=True)
                gates_ref[head : head + 1, :] = by_column
                gates_ref[heads + head : heads + head + 1, :] = jnp.where(seen, grad_log * slope, 0.0)
        if rows_wanted:
            theirs_ref[...] = result_ref[pl.ds(pl.multiple_of((1 - core) * rows, rows), rows), :]

    for side in sides:
        pl.when(chip == side)(functools.partial(part, side))

    if sides == (0,):

        @pl.when(chip != 0)
        def _():
            for source, target in zip(later, (result_ref, theirs_ref, gates_ref)):
                target[...] = source[...]


def hold_kernel(in_ref, out_ref):
    out_ref[...] = in_ref[...]


def near_kernel(qk, vw, length_ref, qg_ref, kv_ref, got_ref, got_out, near_ref, share_ref):
    got_out[...] = got_ref[...]
    heads = got_ref.shape[0] // 2
    size = qg_ref.shape[1]
    wq = heads * qk

    @pl.when(place()[0] == 0)
    def _():
        each = range(heads)
        length = length_ref[0]
        loaded, weights = [], []
        for head in each:
            first = slice(head * qk, (head + 1) * qk)
            second = slice(wq + head * vw, wq + (head + 1) * vw)
            loaded.append((qg_ref[1, :, first], qg_ref[1, :, second], kv_ref[1, :, first], kv_ref[1, :, second]))
            gates = (got_ref[head : head + 1, :], got_ref[heads + head : heads + head + 1, :])
            weights.append(decay(*gates, length, qk**-0.5)[:size, :size])
        scores = [dot(q, k, NT) for q, g, k, v in loaded]
        pulled = [dot(g, v, NT) for q, g, k, v in loaded]
        scores = [scores[head] * weights[head] for head in each]
        norms = [jnp.sum(scores[head], axis=1, keepdims=True) for head in each]
        alongs = [jnp.sum(scores[head] * pulled[head], axis=1, keepdims=True) for head in each]
        terms = [backward_terms(norms[head], alongs[head]) for head in each]
        scaled = [scores[head] * terms[head][0] for head in each]
        grad_raw = [(pulled[head] * terms[head][0] + terms[head][1]) * weights[head] for head in each]
        for head in each:
            q, g, k, v = loaded[head]
            first = slice(head * qk, (head + 1) * qk)
            second = slice(wq + head * vw, wq + (head + 1) * vw)
            near_ref[:, first] = wide_dot(grad_raw[head], k, NN).astype(jnp.bfloat16)
            near_ref[:, second] = wide_dot(scaled[head], v, NN).astype(jnp.bfloat16)
            share_ref[:, first] = wide_dot(grad_raw[head].T, q, NN)
            share_ref[:, second] = wide_dot(scaled[head].T, g, NN)


def merge_kernel(result_a, result_b, got_a, gates_in, *refs):
    *outputs, gates_ref, sems = refs
    core = place()[1]
    rows = got_a.shape[0]
    mine = pl.ds(pl.multiple_of(core * rows, rows), rows)
    pairs = placed(result_a.at[mine, :], outputs, 0, core) + placed(result_b.at[mine, :], outputs, 1, core)
    copies = run_copies(pairs + placed(got_a, outputs, 0, 1 - core), sems)
    gates_ref[...] = gates_in[...]
    for copy in copies:
        copy.wait()


def gates_kernel(gates_a, gates_got, gates_b, gi_ref, gf_ref):
    heads = gi_ref.shape[0]
    gates = jnp.where(place()[0] == 0, gates_a[...] + gates_got[...], gates_b[...])
    gi_ref[...] = gates[:heads]
    gf_ref[...] = gates[heads:]


def last_kernel(got_b, gi_in, gf_in, *refs):
    *outputs, gi_ref, gf_ref, sems = refs[4:]
    pairs = placed(got_b, outputs, 1, 1 - place()[1]) + [(gi_in, gi_ref), (gf_in, gf_ref)]
    for copy in run_copies(pairs, sems):
        copy.wait()


def split_shards(queries, keys, values, cotangent, igate, fgate, lengths):
    rows = queries.shape[0]
    heads = igate.shape[0]
    qk = queries.shape[1] // (4 * heads)
    vw = values.shape[1] // (4 * heads)
    width = heads * (qk + vw)
    bf16, f32 = jnp.bfloat16, jnp.float32
    shape = jax.ShapeDtypeStruct
    vmem = pl.BlockSpec(memory_space=pltpu.VMEM)
    smem = pl.BlockSpec(memory_space=pltpu.SMEM)
    hbm = pl.BlockSpec(memory_space=pltpu.HBM)
    params = pltpu.CompilerParams(vmem_limit_bytes=32 * 1024 * 1024)

    def flops(count):
        return pl.CostEstimate(flops=count, bytes_accessed=0, transcendentals=0)

    costly = flops(4 * 10**10)
    dma = pltpu.SemaphoreType.DMA

    def swap(value, mask):
        return lax.ppermute(value, "head", [(s, s ^ mask) for s in range(4)])

    slots = igate.shape[1]
    gates_shape = shape((2 * heads, slots), f32)
    arrays = [pltpu.with_memory_space_constraint(a, pltpu.HBM) for a in (queries, keys, values, cotangent, igate, fgate)]
    cross_shape = shape((rows, width), bf16)
    a2_sent, gates = pl.pallas_call(
        pack_kernel,
        out_shape=(shape((rows, width + slots), bf16), gates_shape),
        in_specs=[hbm] * 6,
        out_specs=(vmem,) * 2,
        scratch_shapes=[pltpu.VMEM(igate.shape, f32), pltpu.VMEM(igate.shape, f32), dma((4,))],
        compiler_params=params,
    )(*arrays)
    a2 = swap(a2_sent, 2)
    d, to_core = pl.pallas_call(
        more_kernel,
        out_shape=(shape((rows, 2 * width), bf16), shape((rows, 4 * width), bf16)),
        in_specs=[hbm] * 4,
        out_specs=(vmem,) * 2,
        scratch_shapes=[dma((12,))],
        compiler_params=params,
    )(*arrays[:4])
    b2_sent, rest = pl.pallas_call(
        rest_kernel,
        out_shape=(cross_shape, shape((2, rows, width), bf16)),
        in_specs=[hbm] * 4,
        out_specs=(vmem,) * 2,
        scratch_shapes=[dma((6,))],
        compiler_params=params,
    )(*arrays[:4])
    from_core = swap(to_core, 1)
    d = swap(d, 3)
    gates_got = pl.pallas_call(
        join_kernel,
        out_shape=gates_shape,
        in_specs=[vmem],
        out_specs=vmem,
        cost_estimate=costly,
        compiler_params=params,
    )(a2)
    both = shape((2, 2 * rows, width), bf16)
    qg, kv, stats = pl.pallas_call(
        functools.partial(local_kernel, qk, vw),
        out_shape=(both, both, shape((4 * heads, slots), f32)),
        in_specs=[smem] + [vmem] * 6,
        out_specs=(vmem,) * 3,
        cost_estimate=costly,
        compiler_params=params,
    )(lengths, a2_sent, b2_sent, rest, from_core, gates, gates_got)
    stats = swap(stats, 2)
    b2 = swap(b2_sent, 2)
    out_shape = tuple(shape(a.shape, bf16) for a in (queries, keys, values, values))

    results = (shape((2 * rows, 2 * width), bf16), shape((rows, 2 * width), bf16), gates_shape)

    def cross(chunk, sides, work, *received, cost):
        kept = {"gates": results[2:], "rows": results[:2], "all": results}[work]
        return pl.pallas_call(
            functools.partial(cross_kernel, chunk, sides, work, qk, vw),
            out_shape=kept,
            in_specs=[smem] + [vmem] * (4 + len(received)),
            out_specs=(vmem,) * len(kept),
            scratch_shapes=[pltpu.VMEM((4 * rows, width), bf16)],
            cost_estimate=cost,
            compiler_params=params,
        )(lengths, qg, kv, gates, gates_got, *received)

    gates_got, near, share = pl.pallas_call(
        functools.partial(near_kernel, qk, vw),
        out_shape=(gates_shape, shape((2 * rows, width), bf16), shape((2 * rows, width), f32)),
        in_specs=[smem] + [vmem] * 3,
        out_specs=(vmem,) * 3,
        cost_estimate=flops(0),
        compiler_params=params,
    )(lengths, qg, kv, gates_got)
    (gates_later,) = cross(0, (1,), "gates", a2, d, cost=flops(0))
    to_owner = pl.pallas_call(
        hold_kernel,
        out_shape=gates_shape,
        in_specs=[vmem],
        out_specs=vmem,
        cost_estimate=flops(0),
        compiler_params=params,
    )(gates_later)
    gates_back = swap(to_owner, 2)
    later_a = cross(0, (1,), "rows", a2, d, to_owner, cost=flops(0))
    result_a, theirs_a, gates_a = cross(0, (0,), "all", a2, d, stats, *later_a, gates_later, cost=flops(40000000000))
    got_a = swap(theirs_a, 1)
    result_b, theirs_b, gates_b = cross(1, (0, 1), "all", b2, d, stats, near, share, cost=flops(4000000000))
    got_b = swap(theirs_b, 1)
    *outputs, gates_b = pl.pallas_call(
        merge_kernel,
        out_shape=out_shape + (gates_shape,),
        in_specs=[vmem] * 4,
        out_specs=(hbm,) * 4 + (vmem,),
        scratch_shapes=[dma((12,))],
        cost_estimate=flops(0),
        compiler_params=params,
    )(result_a, result_b, got_a, gates_b)
    gate_shape = shape(igate.shape, f32)
    gate_grads = pl.pallas_call(
        gates_kernel,
        out_shape=(gate_shape, gate_shape),
        in_specs=[vmem] * 3,
        out_specs=(vmem,) * 2,
        cost_estimate=costly,
        compiler_params=params,
    )(gates_a, gates_back, gates_b)
    gq, gk, gv, hidden, grad_in, grad_forget = pl.pallas_call(
        last_kernel,
        out_shape=out_shape + (gate_shape, gate_shape),
        in_specs=[vmem] * 3 + [hbm] * 4,
        out_specs=(hbm,) * 6,
        scratch_shapes=[dma((6,))],
        input_output_aliases={3: 0, 4: 1, 5: 2, 6: 3},
        compiler_params=params,
    )(got_b, *gate_grads, *outputs)
    return hidden, gq, gk, gv, grad_in, grad_forget


def shards(*arrays):
    if lax.axis_size("head") == 4:
        return split_shards(*arrays)
    return swapped_shards(*arrays)


def solution(mesh):
    rows = P(("groups", "seq", "head"), None)
    gates = P("head", ("groups", "seq"))
    return jax.shard_map(
        shards,
        mesh=mesh,
        in_specs=(rows, rows, rows, rows, gates, gates, P(("groups", "seq"))),
        out_specs=(rows, rows, rows, rows, gates, gates),
        check_vma=False,
    )
```

```python
import functools

import jax
import jax.numpy as jnp
from jax import lax
from jax.experimental import pallas as pl
from jax.experimental.pallas import tpu as pltpu
from jax.sharding import PartitionSpec as P

FAR = -1e30


def dot(left, right, contract):
    return lax.dot_general(left, right, (contract, ((), ())), preferred_element_type=jnp.float32)


def halves(value):
    high = value.astype(jnp.bfloat16)
    return high, (value - high.astype(jnp.float32)).astype(jnp.bfloat16)


def wide_dot(left, right, contract):
    rows = left.shape[0]
    both = dot(jnp.concatenate(halves(left), axis=0), right, contract)
    return both[:rows] + both[rows:]


NN = ((1,), (0,))
NT = ((1,), (1,))
TN = ((0,), (0,))


def log_sigmoid(value):
    return jnp.minimum(value, 0.0) - jnp.log(1.0 + jnp.exp(-jnp.abs(value)))


def decay(in_gate, forget_gate, length, scale):
    size = in_gate.shape[1]
    rows = lax.broadcasted_iota(jnp.int32, (size, size), 0)
    cols = lax.broadcasted_iota(jnp.int32, (size, size), 1)
    logs = jnp.where(cols[:1] < length, log_sigmoid(forget_gate), 0.0)
    total_col = jnp.sum(jnp.where(cols <= rows, logs, 0.0), axis=1, keepdims=True)
    total_row = jnp.sum(jnp.where(cols == rows, total_col, 0.0), axis=0, keepdims=True)
    mask = (cols <= rows) & (rows < length)
    return jnp.exp(jnp.where(mask, total_col - total_row, FAR)) * (jnp.exp(in_gate) * scale)


def whole_kernel(heads, qk, vw, length_ref, x_ref, ig_ref, fg_ref, out_ref, gi_ref, gf_ref):
    length = length_ref[0]
    size = x_ref.shape[0]
    rows = lax.broadcasted_iota(jnp.int32, (size, size), 0)
    cols = lax.broadcasted_iota(jnp.int32, (size, size), 1)
    for head in range(heads):
        q = x_ref[:, head * qk : (head + 1) * qk]
        k = x_ref[:, (heads + head) * qk : (heads + head + 1) * qk]
        v0 = 2 * heads * qk + head * vw
        g0 = v0 + heads * vw
        v = x_ref[:, v0 : v0 + vw]
        g = x_ref[:, g0 : g0 + vw]
        forget = fg_ref[head : head + 1, :]
        weight = decay(ig_ref[head : head + 1, :], forget, length, qk**-0.5)
        scores = dot(q, k, NT) * weight
        pulled = dot(g, v, NT)
        norm = jnp.sum(scores, axis=1, keepdims=True)
        along = jnp.sum(scores * pulled, axis=1, keepdims=True)
        size_of = jnp.abs(norm)
        inverse = 1.0 / jnp.maximum(size_of, 1.0)
        share = jnp.where(size_of > 1.0, 1.0, jnp.where(size_of == 1.0, 0.5, 0.0))
        grad_norm = -along * inverse * inverse * share * jnp.where(norm < 0.0, -1.0, 1.0)
        grad_scores = pulled * inverse + grad_norm
        hidden = wide_dot(scores * inverse, v, NN)
        grad_raw = grad_scores * weight
        gq = wide_dot(grad_raw, k, NN)
        gk = wide_dot(grad_raw.T, q, NN)
        gv = wide_dot((scores * inverse).T, g, NN)
        out_ref[:, head * qk : (head + 1) * qk] = gq.astype(jnp.bfloat16)
        out_ref[:, (heads + head) * qk : (heads + head + 1) * qk] = gk.astype(jnp.bfloat16)
        out_ref[:, v0 : v0 + vw] = gv.astype(jnp.bfloat16)
        out_ref[:, g0 : g0 + vw] = hidden.astype(jnp.bfloat16)
        by_column = jnp.sum(grad_scores * scores, axis=0, keepdims=True)
        by_row = along * inverse * (1.0 - share)
        moved = by_row - jnp.sum(jnp.where(rows == cols, by_column, 0.0), axis=1, keepdims=True)
        grad_log = jnp.sum(jnp.where(rows >= cols, moved, 0.0), axis=0, keepdims=True)
        gi_ref[head : head + 1, :] = by_column
        gf_ref[head : head + 1, :] = jnp.where(
            cols[:1] < length, grad_log / (1.0 + jnp.exp(forget)), 0.0
        )


def swapped_shards(queries, keys, values, cotangent, igate, fgate, lengths):
    devices = lax.axis_size("head")
    rows = queries.shape[0]
    heads = igate.shape[0]
    qk = queries.shape[1] // (devices * heads)
    vw = values.shape[1] // (devices * heads)
    parts = [a.reshape(rows, devices, -1) for a in (queries, keys, values, cotangent)]
    joined = jnp.concatenate(parts, axis=2)
    here = lax.all_to_all(joined, "head", split_axis=1, concat_axis=0, tiled=True)
    here = here.reshape(rows * devices, -1)
    vmem = pl.BlockSpec(memory_space=pltpu.VMEM)
    out, grad_in, grad_forget = pl.pallas_call(
        functools.partial(whole_kernel, heads, qk, vw),
        out_shape=(
            jax.ShapeDtypeStruct(here.shape, jnp.bfloat16),
            jax.ShapeDtypeStruct(igate.shape, jnp.float32),
            jax.ShapeDtypeStruct(igate.shape, jnp.float32),
        ),
        in_specs=[pl.BlockSpec(memory_space=pltpu.SMEM), vmem, vmem, vmem],
        out_specs=(vmem, vmem, vmem),
        compiler_params=pltpu.CompilerParams(vmem_limit_bytes=32 * 1024 * 1024),
    )(lengths, here, igate, fgate)
    back = lax.all_to_all(
        out.reshape(devices, rows, -1), "head", split_axis=0, concat_axis=0, tiled=True
    )
    back = back.transpose(1, 0, 2)
    ends = [0, heads * qk, 2 * heads * qk, 2 * heads * qk + heads * vw, back.shape[2]]
    gq, gk, gv, hidden = [
        back[:, :, a:b].reshape(rows, -1) for a, b in zip(ends[:-1], ends[1:])
    ]
    return hidden, gq, gk, gv, grad_in, grad_forget


def backward_terms(norm, along):
    size = jnp.abs(norm)
    inverse = 1.0 / jnp.maximum(size, 1.0)
    share = jnp.where(size > 1.0, 1.0, jnp.where(size == 1.0, 0.5, 0.0))
    grad_norm = -along * inverse * inverse * share * jnp.where(norm < 0.0, -1.0, 1.0)
    return inverse, grad_norm, along * inverse * (1.0 - share)


def place():
    me = lax.axis_index("head")
    return me // 2, lax.rem(me, 2)


def run_copies(pairs, sems):
    copies = [pltpu.make_async_copy(a, b, sems.at[i]) for i, (a, b) in enumerate(pairs)]
    for copy in copies:
        copy.start()
    return copies


def block(ref, owner):
    width = ref.shape[1] // 4
    return ref.at[:, pl.ds(pl.multiple_of(owner * width, width), width)]


def block_copies(refs, owner, target):
    split = refs[0].shape[1] // 4
    end = split + refs[1].shape[1] // 4
    return [(block(refs[0], owner), target.at[:, :split]), (block(refs[1], owner), target.at[:, split:end])]


def copy_for_chip(moves, inputs, sems):
    q_ref, k_ref, v_ref, g_ref = inputs
    chip = place()[0]

    @pl.when(chip == 0)
    def _():
        run_copies(moves((k_ref, v_ref), (q_ref, g_ref)), sems)

    @pl.when(chip != 0)
    def _():
        run_copies(moves((q_ref, g_ref), (k_ref, v_ref)), sems)

    pairs = moves((k_ref, v_ref), (q_ref, g_ref))
    return [pltpu.make_async_copy(source, target, sems.at[i]) for i, (source, target) in enumerate(pairs)]


def pack_kernel(q_ref, k_ref, v_ref, g_ref, ig_ref, fg_ref, a2_ref, gates_ref, in_ref, out_ref, sems):
    core = place()[1]
    heads, slots = ig_ref.shape
    width = a2_ref.shape[1] - slots

    def moves(sent, kept):
        return [(ig_ref, in_ref), (fg_ref, out_ref)] + block_copies(sent, core, a2_ref)

    copies = copy_for_chip(moves, (q_ref, k_ref, v_ref, g_ref), sems)
    for copy in copies[:2]:
        copy.wait()
    gates_ref[:heads, :] = in_ref[...]
    gates_ref[heads:, :] = out_ref[...]
    gates = gates_ref[...]
    terms = []
    for _ in range(3):
        terms.append(gates.astype(jnp.bfloat16).astype(jnp.float32))
        gates = gates - terms[-1]
    terms.append(jnp.zeros((a2_ref.shape[0] - 6 * heads, slots), jnp.float32))
    a2_ref[:, width:] = jnp.concatenate(terms, axis=0).astype(jnp.bfloat16)
    for copy in copies[2:]:
        copy.wait()


def more_kernel(q_ref, k_ref, v_ref, g_ref, d_ref, m1_ref, b2_ref, sems):
    core = place()[1]
    width = m1_ref.shape[1] // 4

    def moves(sent, kept):
        pairs = []
        for chunk in range(2):
            pairs += block_copies(sent, 2 * chunk + 1 - core, d_ref.at[:, chunk * width : (chunk + 1) * width])
            for i, refs in enumerate((sent, kept)):
                start = (2 * chunk + i) * width
                pairs += block_copies(refs, 2 * chunk + 1 - core, m1_ref.at[:, start : start + width])
        return pairs + block_copies(sent, 2 + core, b2_ref)

    for copy in copy_for_chip(moves, (q_ref, k_ref, v_ref, g_ref), sems):
        copy.wait()


def rest_kernel(q_ref, k_ref, v_ref, g_ref, rest_ref, sems):
    core = place()[1]

    def moves(sent, kept):
        return block_copies(kept, core, rest_ref.at[0]) + block_copies(kept, 2 + core, rest_ref.at[1])

    for copy in copy_for_chip(moves, (q_ref, k_ref, v_ref, g_ref), sems):
        copy.wait()


def join_kernel(a2_got, got_ref):
    count, slots = got_ref.shape
    terms = a2_got[:, a2_got.shape[1] - slots :].astype(jnp.float32)
    got_ref[...] = terms[:count] + terms[count : 2 * count] + terms[2 * count : 3 * count]


def local_kernel(
    qk, vw, length_ref, a2_ref, b2_ref, rest_ref, m1_ref, own_ref, got_ref, qg_ref, kv_ref, stats_ref
):
    chip, core = place()
    rows = m1_ref.shape[0]
    heads = own_ref.shape[0] // 2
    wq, wv = heads * qk, heads * vw
    width = wq + wv
    mine = pl.ds(pl.multiple_of(core * rows, rows), rows)
    theirs = pl.ds(pl.multiple_of((1 - core) * rows, rows), rows)

    def gather(sent, kept):
        for chunk, own in enumerate((a2_ref, b2_ref)):
            start = chunk * 2 * width
            sent[chunk, mine, :] = own[:, :width]
            sent[chunk, theirs, :] = m1_ref[:, start : start + width]
            kept[chunk, mine, :] = rest_ref[chunk]
            kept[chunk, theirs, :] = m1_ref[:, start + width : start + 2 * width]

    stats_ref[...] = jnp.zeros_like(stats_ref)
    length = length_ref[0]

    def part(side, chunks):
        size = 2 * rows
        low = side * size
        items = [(chunk, head) for chunk in chunks for head in range(heads)]
        scores, pulled = [], []
        for chunk, head in items:
            first = slice(head * qk, (head + 1) * qk)
            second = slice(wq + head * vw, wq + (head + 1) * vw)
            scores.append(dot(qg_ref[chunk, :, first], kv_ref[chunk, :, first], NT))
            pulled.append(dot(qg_ref[chunk, :, second], kv_ref[chunk, :, second], NT))
        for i, (chunk, head) in enumerate(items):
            gates = own_ref if side == chunk else got_ref
            weight = decay(gates[head : head + 1, :], gates[heads + head : heads + head + 1, :], length, qk**-0.5)
            scores[i] = scores[i] * weight[low : low + size, low : low + size]
        norms = [jnp.sum(score, axis=1, keepdims=True) for score in scores]
        alongs = [jnp.sum(score * pull, axis=1, keepdims=True) for score, pull in zip(scores, pulled)]
        on = lax.broadcasted_iota(jnp.int32, (size, 2 * size), 0) + low == lax.broadcasted_iota(
            jnp.int32, (size, 2 * size), 1
        )

        def as_row(column):
            return jnp.sum(jnp.where(on, column, 0.0), axis=0, keepdims=True)

        for (chunk, head), score, pull, norm, along in zip(items, scores, pulled, norms, alongs):
            if side == 1:
                at = chunk * heads + head
                stats_ref[at : at + 1, :] = as_row(norm)
                stats_ref[2 * heads + at : 2 * heads + at + 1, :] = as_row(along)
            else:
                inverse, grad_norm, by_row = backward_terms(norm, along)
                by_column = jnp.sum((pull * inverse + grad_norm) * score, axis=0, keepdims=True)
                stats_ref[head : head + 1, :size] = by_column
                stats_ref[heads + head : heads + head + 1, :] = as_row(by_row)

    @pl.when(chip == 0)
    def _():
        gather(kv_ref, qg_ref)
        part(0, (1,))

    @pl.when(chip != 0)
    def _():
        gather(qg_ref, kv_ref)
        part(1, (0, 1))


def placed(source, targets, chunk, by):
    pairs = []
    start = 0
    for target in targets:
        width = target.shape[1] // 4
        at = pl.ds(pl.multiple_of((2 * chunk + by) * width, width), width)
        pairs.append((source.at[:, start : start + width], target.at[:, at]))
        start += width
    return pairs


def cross_kernel(
    chunk, sides, work, qk, vw, length_ref, qg_ref, kv_ref, own_ref, got_ref, same_ref, other_ref, *refs
):
    chip, core = place()
    rows_wanted, gates_wanted = work != "gates", work != "rows"
    if work == "gates":
        gates_ref, wide_ref = refs
    elif work == "rows":
        _, result_ref, theirs_ref, wide_ref = refs
    elif sides == (0,):
        stats_ref, *later, result_ref, theirs_ref, gates_ref, wide_ref = refs
    else:
        stats_ref, near_ref, share_ref, result_ref, theirs_ref, gates_ref, wide_ref = refs
    rows = other_ref.shape[0]
    size = 2 * rows
    heads = own_ref.shape[0] // 2
    wq, wv = heads * qk, heads * vw

    def gather(side, local):
        base = 0 if side else size
        if side == 1 or chunk == 0:
            wide_ref[side * size : (side + 1) * size, :] = local[chunk]
        for ref, by in ((same_ref, core), (other_ref, 1 - core)):
            start = chunk * (wq + wv) if ref is other_ref else 0
            wide_ref[pl.ds(pl.multiple_of(base + by * rows, rows), rows), :] = ref[:, start : start + wq + wv]

    length = length_ref[0]

    def part(side):
        if gates_wanted:
            gates_ref[...] = jnp.zeros_like(gates_ref)
        gather(side, kv_ref if side else qg_ref)
        thin = (qg_ref if side else kv_ref).at[chunk]
        gates = own_ref if side == chunk else got_ref
        full = 2 * size
        rows_at = lax.broadcasted_iota(jnp.int32, (full, full), 0)
        cols_at = lax.broadcasted_iota(jnp.int32, (full, full), 1)

        def as_column(row):
            return jnp.sum(jnp.where(rows_at == cols_at, row, 0.0), axis=1, keepdims=True)

        weights = [
            decay(gates[head : head + 1, :], gates[heads + head : heads + head + 1, :], length, qk**-0.5)
            for head in range(heads)
        ]
        each = range(heads)
        far = side == 0 and chunk == 1
        loaded = []
        for head in each:
            first = slice(head * qk, (head + 1) * qk)
            second = slice(wq + head * vw, wq + (head + 1) * vw)
            seen = slice(size, 2 * size) if far else slice(None)
            of_wide, of_thin = (wide_ref[seen, first], wide_ref[seen, second]), (thin[:, first], thin[:, second])
            loaded.append(of_wide + of_thin if side == 0 else of_thin + of_wide)
        weights = [weight[:, :size] if side == 0 else weight for weight in weights]
        weights = [weight[size:] if side == 1 or far else weight for weight in weights]
        scores = [dot(q, k, NT) for q, g, k, v in loaded]
        pulled = [dot(g, v, NT) for q, g, k, v in loaded]
        scores = [scores[head] * weights[head] for head in each]
        norms = [jnp.sum(scores[head], axis=1, keepdims=True) for head in each]
        alongs = [jnp.sum(scores[head] * pulled[head], axis=1, keepdims=True) for head in each]
        if side == 0:
            at = chunk * heads
            sums = [as_column(stats_ref[at + head : at + head + 1, :]) for head in each]
            norms = [norms[head] + (sums[head][size:] if far else sums[head]) for head in each]
            at += 2 * heads
            sums = [as_column(stats_ref[at + head : at + head + 1, :]) for head in each]
            alongs = [alongs[head] + (sums[head][size:] if far else sums[head]) for head in each]
        terms = [backward_terms(norms[head], alongs[head]) for head in each]
        grad_scores = [pulled[head] * terms[head][0] + terms[head][1] for head in each]
        if rows_wanted:
            scaled = [scores[head] * terms[head][0] for head in each]
            grad_raw = [grad_scores[head] * weights[head] for head in each]
            turned = [(scaled[head].T, grad_raw[head].T) for head in each]
            if far:
                pass
            elif side == 0:
                scaled, grad_raw = [value[:size] for value in scaled], [value[:size] for value in grad_raw]
            else:
                turned = [(one[size:], other[size:]) for one, other in turned]
            sections = ((0, qk), (wq, qk), (2 * wq, vw), (2 * wq + wv, vw))
            for section, (start, step) in enumerate(sections):
                for head in each:
                    columns = slice(start + head * step, start + (head + 1) * step)
                    if far and section in (0, 3):
                        at = (section // 3) * wq + head * step
                        result_ref[:, columns] = near_ref[:, at : at + step]
                        continue
                    q, g, k, v = loaded[head]
                    left, right = (
                        (grad_raw[head], k), (turned[head][1], q), (turned[head][0], g), (scaled[head], v)
                    )[section]
                    value = wide_dot(left, right, NN)
                    if far:
                        at = (section - 1) * wq + head * step
                        value = value + share_ref[:, at : at + step]
                    result_ref[:, columns] = value.astype(jnp.bfloat16)
        for head in each if gates_wanted else ():
            by_column = jnp.sum(grad_scores[head] * scores[head], axis=0, keepdims=True)
            by_row = terms[head][2]
            forget = gates[heads + head : heads + head + 1, :]
            live = cols_at[:1] < length
            slope = jnp.where(live, 1.0 / (1.0 + jnp.exp(forget)), 0.0)
            if side == 0 and chunk == 0:
                small_rows, small_cols = rows_at[:size, :size], cols_at[:size, :size]
                column = jnp.sum(jnp.where(small_rows == small_cols, by_column, 0.0), axis=1, keepdims=True)
                before = jnp.where(small_rows < small_cols, column - by_row[:size], 0.0)
                grad_log = jnp.sum(before, axis=0, keepdims=True)
                gates_ref[head : head + 1, :size] = by_column
                gates_ref[heads + head : heads + head + 1, :size] = grad_log * slope[:, :size]
            if side == 1:
                row = jnp.sum(jnp.where(rows_at[size:] == cols_at[size:], by_row, 0.0), axis=0, keepdims=True)
                if chunk == 1:
                    by_column = by_column + stats_ref[head : head + 1, :]
                    row = row + stats_ref[heads + head : heads + head + 1, :]
                    seen = jnp.full((1, full), True)
                else:
                    seen = cols_at[:1] >= size
                by_column = jnp.where(seen, by_column, 0.0)
                moved = as_column(row - by_column)
                grad_log = jnp.sum(jnp.where(rows_at >= cols_at, moved, 0.0), axis=0, keepdims=True)
                gates_ref[head : head + 1, :] = by_column
                gates_ref[heads + head : heads + head + 1, :] = jnp.where(seen, grad_log * slope, 0.0)
        if rows_wanted:
            theirs_ref[...] = result_ref[pl.ds(pl.multiple_of((1 - core) * rows, rows), rows), :]

    for side in sides:
        pl.when(chip == side)(functools.partial(part, side))

    if sides == (0,):

        @pl.when(chip != 0)
        def _():
            for source, target in zip(later, (result_ref, theirs_ref, gates_ref)):
                target[...] = source[...]


def hold_kernel(in_ref, out_ref):
    out_ref[...] = in_ref[...]


def near_kernel(qk, vw, length_ref, qg_ref, kv_ref, got_ref, got_out, near_ref, share_ref):
    got_out[...] = got_ref[...]
    heads = got_ref.shape[0] // 2
    size = qg_ref.shape[1]
    wq = heads * qk

    @pl.when(place()[0] == 0)
    def _():
        each = range(heads)
        length = length_ref[0]
        loaded, weights = [], []
        for head in each:
            first = slice(head * qk, (head + 1) * qk)
            second = slice(wq + head * vw, wq + (head + 1) * vw)
            loaded.append((qg_ref[1, :, first], qg_ref[1, :, second], kv_ref[1, :, first], kv_ref[1, :, second]))
            gates = (got_ref[head : head + 1, :], got_ref[heads + head : heads + head + 1, :])
            weights.append(decay(*gates, length, qk**-0.5)[:size, :size])
        scores = [dot(q, k, NT) for q, g, k, v in loaded]
        pulled = [dot(g, v, NT) for q, g, k, v in loaded]
        scores = [scores[head] * weights[head] for head in each]
        norms = [jnp.sum(scores[head], axis=1, keepdims=True) for head in each]
        alongs = [jnp.sum(scores[head] * pulled[head], axis=1, keepdims=True) for head in each]
        terms = [backward_terms(norms[head], alongs[head]) for head in each]
        scaled = [scores[head] * terms[head][0] for head in each]
        grad_raw = [(pulled[head] * terms[head][0] + terms[head][1]) * weights[head] for head in each]
        for head in each:
            q, g, k, v = loaded[head]
            first = slice(head * qk, (head + 1) * qk)
            second = slice(wq + head * vw, wq + (head + 1) * vw)
            near_ref[:, first] = wide_dot(grad_raw[head], k, NN).astype(jnp.bfloat16)
            near_ref[:, second] = wide_dot(scaled[head], v, NN).astype(jnp.bfloat16)
            share_ref[:, first] = wide_dot(grad_raw[head].T, q, NN)
            share_ref[:, second] = wide_dot(scaled[head].T, g, NN)


def merge_kernel(result_a, result_b, got_a, gates_in, *refs):
    *outputs, gates_ref, sems = refs
    core = place()[1]
    rows = got_a.shape[0]
    mine = pl.ds(pl.multiple_of(core * rows, rows), rows)
    pairs = placed(result_a.at[mine, :], outputs, 0, core) + placed(result_b.at[mine, :], outputs, 1, core)
    copies = run_copies(pairs + placed(got_a, outputs, 0, 1 - core), sems)
    gates_ref[...] = gates_in[...]
    for copy in copies:
        copy.wait()


def gates_kernel(gates_a, gates_got, gates_b, gi_ref, gf_ref):
    heads = gi_ref.shape[0]
    gates = jnp.where(place()[0] == 0, gates_a[...] + gates_got[...], gates_b[...])
    gi_ref[...] = gates[:heads]
    gf_ref[...] = gates[heads:]


def last_kernel(got_b, gi_in, gf_in, *refs):
    *outputs, gi_ref, gf_ref, sems = refs[4:]
    pairs = placed(got_b, outputs, 1, 1 - place()[1]) + [(gi_in, gi_ref), (gf_in, gf_ref)]
    for copy in run_copies(pairs, sems):
        copy.wait()


def split_shards(queries, keys, values, cotangent, igate, fgate, lengths):
    rows = queries.shape[0]
    heads = igate.shape[0]
    qk = queries.shape[1] // (4 * heads)
    vw = values.shape[1] // (4 * heads)
    width = heads * (qk + vw)
    bf16, f32 = jnp.bfloat16, jnp.float32
    shape = jax.ShapeDtypeStruct
    vmem = pl.BlockSpec(memory_space=pltpu.VMEM)
    smem = pl.BlockSpec(memory_space=pltpu.SMEM)
    hbm = pl.BlockSpec(memory_space=pltpu.HBM)
    params = pltpu.CompilerParams(vmem_limit_bytes=32 * 1024 * 1024)

    def flops(count):
        return pl.CostEstimate(flops=count, bytes_accessed=0, transcendentals=0)

    costly = flops(4 * 10**10)
    dma = pltpu.SemaphoreType.DMA

    def swap(value, mask):
        return lax.ppermute(value, "head", [(s, s ^ mask) for s in range(4)])

    slots = igate.shape[1]
    gates_shape = shape((2 * heads, slots), f32)
    arrays = [pltpu.with_memory_space_constraint(a, pltpu.HBM) for a in (queries, keys, values, cotangent, igate, fgate)]
    cross_shape = shape((rows, width), bf16)
    a2_sent, gates = pl.pallas_call(
        pack_kernel,
        out_shape=(shape((rows, width + slots), bf16), gates_shape),
        in_specs=[hbm] * 6,
        out_specs=(vmem,) * 2,
        scratch_shapes=[pltpu.VMEM(igate.shape, f32), pltpu.VMEM(igate.shape, f32), dma((4,))],
        compiler_params=params,
    )(*arrays)
    a2 = swap(a2_sent, 2)
    d, to_core, b2_sent = pl.pallas_call(
        more_kernel,
        out_shape=(shape((rows, 2 * width), bf16), shape((rows, 4 * width), bf16), cross_shape),
        in_specs=[hbm] * 4,
        out_specs=(vmem,) * 3,
        scratch_shapes=[dma((14,))],
        compiler_params=params,
    )(*arrays[:4])
    rest = pl.pallas_call(
        rest_kernel,
        out_shape=shape((2, rows, width), bf16),
        in_specs=[hbm] * 4,
        out_specs=vmem,
        scratch_shapes=[dma((4,))],
        compiler_params=params,
    )(*arrays[:4])
    from_core = swap(to_core, 1)
    d = swap(d, 3)
    gates_got = pl.pallas_call(
        join_kernel,
        out_shape=gates_shape,
        in_specs=[vmem],
        out_specs=vmem,
        cost_estimate=costly,
        compiler_params=params,
    )(a2)
    both = shape((2, 2 * rows, width), bf16)
    qg, kv, stats = pl.pallas_call(
        functools.partial(local_kernel, qk, vw),
        out_shape=(both, both, shape((4 * heads, slots), f32)),
        in_specs=[smem] + [vmem] * 6,
        out_specs=(vmem,) * 3,
        cost_estimate=costly,
        compiler_params=params,
    )(lengths, a2_sent, b2_sent, rest, from_core, gates, gates_got)
    stats = swap(stats, 2)
    b2 = swap(b2_sent, 2)
    out_shape = tuple(shape(a.shape, bf16) for a in (queries, keys, values, values))

    results = (shape((2 * rows, 2 * width), bf16), shape((rows, 2 * width), bf16), gates_shape)

    def cross(chunk, sides, work, *received, cost):
        kept = {"gates": results[2:], "rows": results[:2], "all": results}[work]
        return pl.pallas_call(
            functools.partial(cross_kernel, chunk, sides, work, qk, vw),
            out_shape=kept,
            in_specs=[smem] + [vmem] * (4 + len(received)),
            out_specs=(vmem,) * len(kept),
            scratch_shapes=[pltpu.VMEM((4 * rows, width), bf16)],
            cost_estimate=cost,
            compiler_params=params,
        )(lengths, qg, kv, gates, gates_got, *received)

    gates_got, near, share = pl.pallas_call(
        functools.partial(near_kernel, qk, vw),
        out_shape=(gates_shape, shape((2 * rows, width), bf16), shape((2 * rows, width), f32)),
        in_specs=[smem] + [vmem] * 3,
        out_specs=(vmem,) * 3,
        cost_estimate=flops(0),
        compiler_params=params,
    )(lengths, qg, kv, gates_got)
    (gates_later,) = cross(0, (1,), "gates", a2, d, cost=flops(0))
    to_owner = pl.pallas_call(
        hold_kernel,
        out_shape=gates_shape,
        in_specs=[vmem],
        out_specs=vmem,
        cost_estimate=flops(0),
        compiler_params=params,
    )(gates_later)
    gates_back = swap(to_owner, 2)
    later_a = cross(0, (1,), "rows", a2, d, to_owner, cost=flops(0))
    result_a, theirs_a, gates_a = cross(0, (0,), "all", a2, d, stats, *later_a, gates_later, cost=flops(40000000000))
    got_a = swap(theirs_a, 1)
    result_b, theirs_b, gates_b = cross(1, (0, 1), "all", b2, d, stats, near, share, cost=flops(4000000000))
    got_b = swap(theirs_b, 1)
    *outputs, gates_b = pl.pallas_call(
        merge_kernel,
        out_shape=out_shape + (gates_shape,),
        in_specs=[vmem] * 4,
        out_specs=(hbm,) * 4 + (vmem,),
        scratch_shapes=[dma((12,))],
        cost_estimate=flops(0),
        compiler_params=params,
    )(result_a, result_b, got_a, gates_b)
    gate_shape = shape(igate.shape, f32)
    gate_grads = pl.pallas_call(
        gates_kernel,
        out_shape=(gate_shape, gate_shape),
        in_specs=[vmem] * 3,
        out_specs=(vmem,) * 2,
        cost_estimate=costly,
        compiler_params=params,
    )(gates_a, gates_back, gates_b)
    gq, gk, gv, hidden, grad_in, grad_forget = pl.pallas_call(
        last_kernel,
        out_shape=out_shape + (gate_shape, gate_shape),
        in_specs=[vmem] * 3 + [hbm] * 4,
        out_specs=(hbm,) * 6,
        scratch_shapes=[dma((6,))],
        input_output_aliases={3: 0, 4: 1, 5: 2, 6: 3},
        compiler_params=params,
    )(got_b, *gate_grads, *outputs)
    return hidden, gq, gk, gv, grad_in, grad_forget


def shards(*arrays):
    if lax.axis_size("head") == 4:
        return split_shards(*arrays)
    return swapped_shards(*arrays)


def solution(mesh):
    rows = P(("groups", "seq", "head"), None)
    gates = P("head", ("groups", "seq"))
    return jax.shard_map(
        shards,
        mesh=mesh,
        in_specs=(rows, rows, rows, rows, gates, gates, P(("groups", "seq"))),
        out_specs=(rows, rows, rows, rows, gates, gates),
        check_vma=False,
    )
```
